256 devices in a mesh: dp: 32 (over x, z), grp: 8 (over y, core).
Axes of the slice: x: 4, y: 4, z: 8, core: 2. Of those that a mesh axis runs over, the one named last changes fastest.
Arguments:
- q_latent: bfloat16 [4096, 128, 512], P(('grp', 'dp')), parts along dimension 0, may hold values from -60 to 60, as said below
- q_rope: bfloat16 [4096, 64, 128], P(('grp', 'dp')), parts along dimension 0, may hold values from -6 to 6
- cache_latent: bfloat16 [4096, 512, 512], P(('grp', 'dp')), parts along dimension 0, may hold values from -6 to 6
- rope_keys: bfloat16 [4096, 64, 512], P(('grp', 'dp')), parts along dimension 0, may hold values from -6 to 6
- lengths: int32 [4096], P(('grp', 'dp')), parts along dimension 0, may hold values from 1 to 512, as said below
- counts: int32 [256], P(('grp', 'dp')), parts along dimension 0, may hold values from 1 to 16, as said below
- w_uv: bfloat16 [128, 512, 128], P('dp'), may hold values from -0.5 to 0.5
- w_o: bfloat16 [16384, 7168], P('dp'), may hold values from -0.1875 to 0.1875
- residual: bfloat16 [4096, 7168], P(('grp', 'dp')), parts along dimension 0, may hold values from -6 to 6
- norm_gain: bfloat16 [7168], replicated, may hold values from 0.25 to 1.75
Outputs:
- hidden_state: bfloat16 [4096, 7168], P(('grp', 'dp')), parts along dimension 0
- mlp_input: bfloat16 [4096, 7168], P(('grp', 'dp')), parts along dimension 0
The draws below stay inside these ranges and needn't reach their ends.
There are 8 independent parts, one for each index of `grp`. The reference program is written for one: setup_inputs(seed, part) draws one part's arguments, and reference() takes and returns one part's arrays. A program takes and returns all parts, laid end to end along the dimension named above; an argument that names none is the same for every part. Nothing has to cross between parts.
Inputs may be any that keep to these rules, and one draw needn't show every extreme that they name: `lengths`: each slot's context length; in each group some slot holds exactly 512. Lengths differ strongly from device to device. Slots 0 to counts - 1 of a device hold live requests; in each group some device is full. `q_latent`: query entries within -60 to 60.
All inputs are finite; a program needn't handle non-finite values.
Results may differ from the reference program's by a relative error of at most 0.025.
Values may be sent and summed in bfloat16 or wider, within the bound.
A program may use at most 128 MiB of HBM per device.

```python
import jax
import jax.numpy as jnp
from jax import lax

D = 7168
H = 128
LAT = 512
ROPE = 64
VDIM = 128
SLOTS = 16
CTX = 512
ROWS = 512
HEADS_DEV = 4
N_DP = 32


def shared_rows(key):
    return jnp.clip(jax.random.normal(key, (ROWS, 2, LAT), jnp.float32), -6.0, 6.0)


def draw_cache_latent(key, part):
    first = shared_rows(key)
    key = jax.random.fold_in(key, 3)
    rest = jnp.clip(jax.random.normal(key, (ROWS, CTX - 2, LAT), jnp.float32), -6.0, 6.0)
    return jnp.concatenate([first, rest], axis=1).astype(jnp.bfloat16)


def draw_q_latent(key, part):
    key = jax.random.fold_in(key, 5)
    base = jnp.clip(jax.random.normal(key, (ROWS, H, LAT), jnp.float32), -6.0, 6.0)
    return base.astype(jnp.bfloat16)


def draw_lengths(key, part):
    key = jax.random.fold_in(key, 13)
    raw_len = jax.random.randint(jax.random.fold_in(key, 1), (ROWS,), 1, CTX + 1)
    shifts = jnp.repeat(jax.random.randint(jax.random.fold_in(key, 2), (N_DP,), 0, 4), SLOTS)
    values = jnp.maximum(jnp.right_shift(raw_len, shifts), 1)
    chosen = jax.random.randint(jax.random.fold_in(key, 3), (), 0, ROWS)
    return values.at[chosen].set(CTX).astype(jnp.int32)


def draw_counts(key, part):
    key = jax.random.fold_in(key, 17)
    values = jax.random.randint(jax.random.fold_in(key, 1), (N_DP,), 1, SLOTS + 1)
    chosen = jax.random.randint(jax.random.fold_in(key, 2), (), 0, N_DP)
    return values.at[chosen].set(SLOTS).astype(jnp.int32)


def shard_levels(stream_key, dims, pieces, smallest, top_value):
    loudness, own = 1.0, jax.random.fold_in(stream_key, 6)
    for axis_at, parts in pieces:
        steps = jnp.exp(jax.random.uniform(jax.random.fold_in(own, axis_at), (parts,), jnp.float32, smallest / len(pieces), top_value / len(pieces)))
        loudness = loudness * jnp.repeat(steps, dims[axis_at] // parts).reshape([-1 if axis == axis_at else 1 for axis in range(len(dims))])
    return loudness


def bell_draw(stream_key, extent, deviation, reach, pieces=(), kind=jnp.bfloat16):
    result = jax.random.normal(stream_key, extent, jnp.float32) * deviation
    if len(pieces) > 0:
        result = shard_levels(stream_key, extent, pieces, -0.22, 0.18) * result
    return jnp.clip(result, min=-reach, max=reach).astype(kind)


def setup_inputs(seed: int = 0, part: int = 0) -> dict:
    seeds = jax.random.split(jax.random.key(seed), 11)
    part_splits = jax.random.split(jax.random.fold_in(seeds[10], part), 11)
    q_latent = draw_q_latent(jax.random.fold_in(jax.random.fold_in(seeds[10], part), 71), part)
    q_rope = bell_draw(part_splits[1], (ROWS, ROPE, H), 1.0, 6.0, ((0, 32),))
    cache_latent = draw_cache_latent(jax.random.fold_in(jax.random.fold_in(seeds[10], part), 71), part)
    rope_keys = bell_draw(part_splits[3], (ROWS, ROPE, CTX), 1.0, 6.0, ((0, 32),))
    lengths = draw_lengths(jax.random.fold_in(jax.random.fold_in(seeds[10], part), 71), part)
    counts = draw_counts(jax.random.fold_in(jax.random.fold_in(seeds[10], part), 71), part)
    w_uv = bell_draw(seeds[6], (H, LAT, VDIM), (LAT // 4) ** -0.5, 0.5, ((0, 32),))
    w_o = bell_draw(seeds[7], (H * VDIM, D), (H * VDIM // 16) ** -0.5, 0.1875, ((0, 32),))
    residual = bell_draw(part_splits[8], (ROWS, D), 1.0, 6.0, ((0, 32),))
    norm_gain = jnp.clip(1.0 + 0.15 * jax.random.normal(seeds[9], (D,), jnp.float32), 0.25, 1.75).astype(jnp.bfloat16)
    return {"q_latent": q_latent, "q_rope": q_rope, "cache_latent": cache_latent, "rope_keys": rope_keys, "lengths": lengths, "counts": counts, "w_uv": w_uv, "w_o": w_o, "residual": residual, "norm_gain": norm_gain}


score_scale = 192.0 ** (-0.5)
norm_eps = 1e-06

def attend_slot(operands):
    query, query_rope, latents, rope_cache, length = operands
    scores = jnp.dot(query, latents.T, preferred_element_type=jnp.float32)
    scores = scores + jnp.dot(query_rope.T, rope_cache, preferred_element_type=jnp.float32)
    scores = scores * score_scale
    positions = jnp.arange(CTX, dtype=jnp.int32)
    visible = (positions < length)[None, :]
    scores = jnp.where(visible, scores, jnp.float32(-1e+30))
    row_max = lax.optimization_barrier(jnp.max(scores, axis=1, keepdims=True))
    expos = jnp.where(visible, jnp.exp(scores - row_max), jnp.float32(0.0))
    probs = (expos / lax.optimization_barrier(jnp.sum(expos, axis=1, keepdims=True))).astype(jnp.bfloat16)
    return jnp.dot(probs, latents, preferred_element_type=jnp.float32).astype(jnp.bfloat16)

def reference(q_latent, q_rope, cache_latent, rope_keys, lengths, counts, w_uv, w_o, residual, norm_gain):
    latent_out = lax.map(attend_slot, (q_latent, q_rope, cache_latent, rope_keys, lengths))
    head_values = jnp.einsum('rhk,hkd->rhd', latent_out.astype(jnp.float32), w_uv.astype(jnp.float32)).astype(jnp.bfloat16)
    block_width = HEADS_DEV * VDIM
    value_blocks = jnp.transpose(head_values.reshape(ROWS, N_DP, block_width), (1, 0, 2))
    weight_blocks = w_o.reshape(N_DP, block_width, D)

    def add_block(total, operands):
        values, weights = operands
        partial_value = jnp.dot(values, weights, preferred_element_type=jnp.float32).astype(jnp.bfloat16)
        return (total + partial_value.astype(jnp.float32), None)
    projected, _ = lax.scan(add_block, jnp.zeros((ROWS, D), jnp.float32), (value_blocks, weight_blocks))
    slot_ids = jnp.arange(ROWS, dtype=jnp.int32)
    live_rows = (slot_ids % SLOTS < counts[slot_ids // SLOTS]).astype(jnp.float32)
    hidden_state = (residual.astype(jnp.float32) + live_rows[:, None] * projected).astype(jnp.bfloat16)
    hidden_f = hidden_state.astype(jnp.float32)
    inv_rms = lax.rsqrt(lax.optimization_barrier(jnp.mean(hidden_f * hidden_f, axis=1, keepdims=True)) + norm_eps)
    mlp_input = (hidden_f * inv_rms * norm_gain.astype(jnp.float32)[None, :]).astype(jnp.bfloat16)
    return (hidden_state, mlp_input)
```

```python
import jax
import jax.numpy as jnp
from jax import lax
from jax.experimental import pallas as pl
from jax.experimental.pallas import tpu as pltpu
from jax.sharding import PartitionSpec as P

score_scale = 192.0 ** (-0.5)
norm_eps = 1e-06

NX, NZ = 4, 8
SLOTS = 16
WIDTH = 7168
DEPTH = 512
COLS = 256
XW, ZW = 1024, 768
MESH = pl.DeviceIdType.MESH
F32, BF16 = jnp.float32, jnp.bfloat16


def hops(size, kind):
    long, short = size // 2, size // 2 - 1
    return (long, short) if kind == 0 else (short, long)


def project_kernel(
    hv_ref, wo_ref, res_ref, gain_ref, counts_ref, hid_ref, mlp_ref,
    wo, px, pz, rx1, rx2, rz1, rz2, acc, load_sem, send_sem, recv_sem,
):
    dp, grp = lax.axis_index("dp"), lax.axis_index("grp")
    x, z = dp // NZ, dp % NZ

    def at_x(step):
        return (x + step + NX) % NX

    def at_z(step):
        return (z + step + NZ) % NZ

    def device(dx, dz):
        return (at_x(dx) * NZ + at_z(dz), grp)

    streams = []
    for i in range(4):
        streams.append((True, i, i % 2, i * XW, XW))
        streams.append((False, i, i % 2, 4 * XW + i * ZW, ZW))
    loads = []
    for n, (_, _, _, first, width) in enumerate(streams):
        load = pltpu.make_async_copy(
            wo_ref.at[:, pl.ds(first, width)], wo.at[:, pl.ds(first, width)], load_sem.at[n]
        )
        load.start()
        loads.append(load)

    barrier = pltpu.get_barrier_semaphore()
    for dx, dz in ((1, 0), (-1, 0), (0, 1), (0, -1)):
        pl.semaphore_signal(barrier, inc=1, device_id=device(dx, dz), device_id_type=MESH)
    pl.semaphore_wait(barrier, 4)

    copies = {}

    def send(n, phase, way, hop):
        along_x, i, kind, _, _ = streams[n]
        axis_x = along_x == (phase == 0)
        size = NX if axis_x else NZ
        right, left = hops(size, kind)
        step = right - hop if way == 0 else hop - left
        slot = hop if way == 0 else right + hop
        if along_x:
            part = px.at[i, at_x(step)] if phase == 0 else px.at[i, x, at_z(step)]
            land = rx1.at[i, slot] if phase == 0 else rx2.at[i, slot]
        else:
            part = pz.at[i, :, at_z(step)] if phase == 0 else pz.at[i, at_x(step), z]
            land = rz1.at[i, slot] if phase == 0 else rz2.at[i, slot]
        move = 1 if way == 0 else -1
        copy = pltpu.make_async_remote_copy(
            src_ref=part,
            dst_ref=land,
            send_sem=send_sem.at[len(copies)],
            recv_sem=recv_sem.at[len(copies)],
            device_id=device(move, 0) if axis_x else device(0, move),
            device_id_type=MESH,
        )
        if hop > 0:
            copies[n, phase, way, hop - 1][0].wait_recv()
            before = copies[n, phase, way, hop - 1][1]
            part[...] = (before[...].astype(F32) + part[...].astype(F32)).astype(BF16)
        copy.start()
        copies[n, phase, way, hop] = (copy, land)

    def first_hops(n, phase):
        for way in (0, 1):
            send(n, phase, way, 0)

    def next_hops(n, phase, hop):
        along_x, _, kind, _, _ = streams[n]
        count = hops(NX if along_x == (phase == 0) else NZ, kind)
        for way in (0, 1):
            if hop < count[way]:
                send(n, phase, way, hop)

    def arrivals(n, phase):
        along_x, _, kind, _, _ = streams[n]
        count = hops(NX if along_x == (phase == 0) else NZ, kind)
        total = None
        for way in (0, 1):
            copy, land = copies[n, phase, way, count[way] - 1]
            copy.wait_recv()
            total = land[...].astype(F32) if total is None else total + land[...].astype(F32)
        return total

    def turn(n):
        along_x, i, _, _, _ = streams[n]
        total = arrivals(n, 0)
        mine = px.at[i, x] if along_x else pz.at[i, :, z]
        mine[...] = (mine[...].astype(F32) + total).astype(BF16)
        first_hops(n, 1)

    live = (
        lax.broadcasted_iota(jnp.int32, (SLOTS, 1), 0) < counts_ref[0]
    ).astype(F32)

    def finish(n):
        along_x, i, _, first, width = streams[n]
        total = arrivals(n, 1)
        mine = px.at[i, x, z] if along_x else pz.at[i, x, z]
        total = total + mine[...].astype(F32)
        where = pl.ds(first, width)
        hidden = (res_ref[:, where].astype(F32) + live * total).astype(BF16)
        hid_ref[:, where] = hidden
        hidden = hidden.astype(F32)
        acc[...] += jnp.sum(hidden * hidden, axis=1, keepdims=True)

    acc[...] = jnp.zeros_like(acc)
    for n, (along_x, i, _, first, width) in enumerate(streams):
        loads[n].wait()
        part = px if along_x else pz

        @pl.loop(0, width // COLS)
        def _(tile):
            off = pl.multiple_of(tile * COLS, COLS)
            out = jnp.dot(
                hv_ref[...], wo[:, pl.ds(first + off, COLS)], preferred_element_type=F32
            )
            part[i, :, :, :, pl.ds(off, COLS)] = out.astype(BF16).reshape(NX, NZ, SLOTS, COLS)

        first_hops(n, 0)

    X, Z = (0, 2, 4, 6), (1, 3, 5, 7)
    plan = [
        (next_hops, Z[0], 0, 1), (next_hops, X[0], 0, 1), (next_hops, Z[1], 0, 1),
        (next_hops, Z[2], 0, 1), (next_hops, X[1], 0, 1), (next_hops, Z[3], 0, 1),
        (next_hops, Z[0], 0, 2), (next_hops, Z[1], 0, 2), (next_hops, X[2], 0, 1),
        (next_hops, Z[2], 0, 2), (next_hops, Z[3], 0, 2),
        (turn, X[0]), (next_hops, X[3], 0, 1), (next_hops, Z[0], 0, 3), (next_hops, Z[1], 0, 3),
        (turn, X[1]), (next_hops, X[0], 1, 1),
        (next_hops, Z[2], 0, 3), (next_hops, Z[3], 0, 3),
        (next_hops, X[1], 1, 1), (next_hops, X[0], 1, 2), (turn, Z[0]), (turn, Z[1]),
        (next_hops, X[1], 1, 2), (next_hops, X[0], 1, 3), (next_hops, X[1], 1, 3),
        (turn, X[2]), (turn, Z[2]), (turn, Z[3]), (turn, X[3]),
        (next_hops, Z[0], 1, 1), (next_hops, Z[1], 1, 1),
        (next_hops, X[2], 1, 1), (next_hops, X[3], 1, 1),
        (next_hops, Z[2], 1, 1), (next_hops, Z[3], 1, 1),
        (next_hops, X[2], 1, 2), (next_hops, X[3], 1, 2),
        (finish, X[0]), (finish, X[1]),
        (next_hops, X[2], 1, 3), (next_hops, X[3], 1, 3),
        (finish, Z[0]), (finish, Z[1]), (finish, Z[2]), (finish, Z[3]),
        (finish, X[2]), (finish, X[3]),
    ]
    for act, *rest in plan:
        act(*rest)

    inv = lax.rsqrt(acc[...] * (1.0 / WIDTH) + norm_eps)
    mlp_ref[...] = (hid_ref[...].astype(F32) * inv * gain_ref[...].astype(F32)).astype(BF16)
    for copy, _ in copies.values():
        copy.wait_send()


def project(flat_values, w_o, residual, norm_gain, counts):
    vmem = pl.BlockSpec(memory_space=pltpu.VMEM)
    count = 8 * 10
    return pl.pallas_call(
        project_kernel,
        out_shape=[jax.ShapeDtypeStruct((SLOTS, WIDTH), BF16)] * 2,
        in_specs=[
            vmem, pl.BlockSpec(memory_space=pl.ANY), vmem, vmem,
            pl.BlockSpec(memory_space=pltpu.SMEM),
        ],
        out_specs=[vmem, vmem],
        scratch_shapes=[
            pltpu.VMEM((DEPTH, WIDTH), BF16),
            pltpu.VMEM((4, NX, NZ, SLOTS, XW), BF16),
            pltpu.VMEM((4, NX, NZ, SLOTS, ZW), BF16),
            pltpu.VMEM((4, 3, NZ, SLOTS, XW), BF16),
            pltpu.VMEM((4, 7, SLOTS, XW), BF16),
            pltpu.VMEM((4, 7, NX, SLOTS, ZW), BF16),
            pltpu.VMEM((4, 3, SLOTS, ZW), BF16),
            pltpu.VMEM((SLOTS, 1), F32),
            pltpu.SemaphoreType.DMA((8,)),
            pltpu.SemaphoreType.DMA((count,)),
            pltpu.SemaphoreType.DMA((count,)),
        ],
        compiler_params=pltpu.CompilerParams(
            collective_id=0, has_side_effects=True, vmem_limit_bytes=48 * 1024 * 1024
        ),
        cost_estimate=pl.CostEstimate(
            flops=2 * 512 * 512 * 7168, bytes_accessed=8 * 1024 * 1024, transcendentals=0
        ),
    )(flat_values, w_o, residual, norm_gain.reshape(1, WIDTH), counts)


def body(
    q_latent, q_rope, cache_latent, rope_keys, lengths, counts, w_uv, w_o, residual, norm_gain
):
    slot_count = q_latent.shape[0]
    context = cache_latent.shape[1]
    scores = jnp.einsum("shk,stk->sht", q_latent, cache_latent, preferred_element_type=jnp.float32)
    scores = scores + jnp.einsum(
        "sjh,sjt->sht", q_rope, rope_keys, preferred_element_type=jnp.float32
    )
    scores = scores * score_scale
    positions = lax.broadcasted_iota(jnp.int32, (slot_count, 1, context), 2)
    visible = positions < lengths[:, None, None]
    scores = jnp.where(visible, scores, jnp.float32(-1e30))
    row_max = jnp.max(scores, axis=2, keepdims=True)
    expos = jnp.where(visible, jnp.exp(scores - row_max), jnp.float32(0.0))
    probs = (expos / jnp.sum(expos, axis=2, keepdims=True)).astype(jnp.bfloat16)
    latent_out = jnp.einsum(
        "sht,stk->shk", probs, cache_latent, preferred_element_type=jnp.float32
    ).astype(jnp.bfloat16)
    routed = lax.all_to_all(latent_out, "dp", split_axis=1, concat_axis=0, tiled=True)
    head_values = jnp.einsum(
        "rhk,hkd->rhd", routed, w_uv, preferred_element_type=jnp.float32
    ).astype(jnp.bfloat16)
    flat_values = head_values.reshape(head_values.shape[0], -1)
    return tuple(project(flat_values, w_o, residual, norm_gain, counts))


def solution(mesh):
    in_specs = (
        P(("grp", "dp"), None, None),
        P(("grp", "dp"), None, None),
        P(("grp", "dp"), None, None),
        P(("grp", "dp"), None, None),
        P(("grp", "dp")),
        P(("grp", "dp")),
        P("dp", None, None),
        P("dp", None),
        P(("grp", "dp"), None),
        P(),
    )
    out_specs = (P(("grp", "dp"), None), P(("grp", "dp"), None))
    return jax.shard_map(body, mesh=mesh, in_specs=in_specs, out_specs=out_specs, check_vma=False)
```

```python
import jax
import jax.numpy as jnp
from jax import lax
from jax.experimental import pallas as pl
from jax.experimental.pallas import tpu as pltpu
from jax.sharding import PartitionSpec as P

score_scale = 192.0 ** (-0.5)
log2_e = 1.4426950408889634
norm_eps = 1e-06

NX, NZ = 4, 8
SLOTS = 16
HEADS, LAT, VDIM, ROPE, CTX = 128, 512, 128, 64, 512
OWN = 4
WIDTH = 7168
DEPTH = OWN * VDIM
COLS = 256
GROUP = 2
LANES = 128
XW, ZW = 1024, 768
MESH = pl.DeviceIdType.MESH
F32, BF16 = jnp.float32, jnp.bfloat16


def hops(size, kind):
    long, short = size // 2, size // 2 - 1
    return (long, short) if kind == 0 else (short, long)


def decode_kernel(
    q_hbm, qr_hbm, cache_hbm, rope_hbm, wuv_hbm, wo_hbm, lengths_ref, counts_ref, res_ref, gain_ref,
    hid_ref, mlp_ref,
    q_ref, qr_ref, cache_ref, rope_ref, lat32, lat_out, lat_in, wuv, hv_out, hv,
    wo, px, pz, rx1, rx2, rz1, rz2, acc,
    slot_sem, uv_sem, load_sem,
    ring_send, ring_recv, pair_send, pair_recv, lat_send, lat_recv, hv_send, hv_recv, send_sem, recv_sem,
):
    dp, grp = lax.axis_index("dp"), lax.axis_index("grp")
    x, z = dp // NZ, dp % NZ
    core = grp % 2
    sign = 1 - 2 * core
    sibling = (dp, grp + sign)

    def at_x(step):
        return (x + step + NX) % NX

    def at_z(step):
        return (z + step + NZ) % NZ

    def device(dx, dz):
        return (at_x(dx) * NZ + at_z(dz), grp)

    started = []

    def remote(src, dst, sends, recvs, index, target):
        copy = pltpu.make_async_remote_copy(
            src_ref=src, dst_ref=dst, send_sem=sends.at[index], recv_sem=recvs.at[index],
            device_id=target, device_id_type=MESH,
        )
        copy.start()
        started.append(copy)
        return copy

    barrier = pltpu.get_barrier_semaphore()
    peers = [device(d, 0) for d in range(1, NX)] + [device(0, d) for d in range(1, NZ)] + [sibling]
    for peer in peers:
        pl.semaphore_signal(barrier, inc=1, device_id=peer, device_id_type=MESH)

    uv_load = pltpu.make_async_copy(wuv_hbm, wuv.at[z], uv_sem)
    uv_load.start()

    def slot_loads(group):
        where = pl.ds(group * GROUP, GROUP)
        return [
            pltpu.make_async_copy(hbm.at[where], vmem.at[where], slot_sem.at[n, group])
            for n, (hbm, vmem) in enumerate(
                ((q_hbm, q_ref), (cache_hbm, cache_ref), (qr_hbm, qr_ref), (rope_hbm, rope_ref))
            )
        ]

    for group in range(SLOTS // GROUP):
        for load in slot_loads(group):
            load.start()

    streams = []
    for i in range(4):
        streams.append((True, i, i % 2, i * XW, XW))
        streams.append((False, i, i % 2, 4 * XW + i * ZW, ZW))
    loads = []
    for n, (_, _, _, first, width) in enumerate(streams):
        load = pltpu.make_async_copy(
            wo_hbm.at[:, pl.ds(first, width)], wo.at[:, pl.ds(first, width)], load_sem.at[n]
        )
        load.start()
        loads.append(load)

    position = lax.broadcasted_iota(jnp.int32, (1, CTX), 1)

    def attend(slot):
        scores = lax.dot_general(
            q_ref[slot], cache_ref[slot], (((1,), (1,)), ((), ())), preferred_element_type=F32
        )
        scores += lax.dot_general(
            qr_ref[slot], rope_ref[slot], (((0,), (0,)), ((), ())), preferred_element_type=F32
        )
        scores = jnp.where(position < lengths_ref[slot], scores, -1e30)
        top = jnp.max(scores, axis=1, keepdims=True)
        expos = jnp.exp2((scores - top) * (score_scale * log2_e))
        probs = (expos * (1.0 / jnp.sum(expos, axis=1, keepdims=True))).astype(BF16)
        rows = pl.ds(pl.multiple_of(slot * HEADS, HEADS), HEADS)
        latents = jnp.dot(probs, cache_ref[slot], preferred_element_type=F32)
        for k in range(LAT // LANES):
            lat32[k, rows, :] = latents[:, k * LANES : (k + 1) * LANES]

    def attend_groups(first, last):
        @pl.loop(first, last)
        def _(group):
            for load in slot_loads(group):
                load.wait()
            for j in range(GROUP):
                attend(group * GROUP + j)

    ring_hops = (NZ // 2, NZ // 2 - 1)
    ring, pair = {}, {}

    def origin(way, hop):
        return at_z(hop * (-sign if way == 0 else sign))

    def ring_send_hop(way, hop):
        to = (x * NZ + at_z(sign if way == 0 else -sign), grp)
        for k in range(2):
            piece = wuv.at[origin(way, hop), core * 2 + k]
            index = (way * 4 + hop) * 2 + k
            ring[way, hop, k] = remote(piece, piece, ring_send, ring_recv, index, to)

    def ring_step(hop):
        for way in (0, 1):
            if hop >= ring_hops[way]:
                continue
            for k in range(2):
                ring[way, hop, k].wait_recv()
            if hop + 1 < ring_hops[way]:
                ring_send_hop(way, hop + 1)
            for k in range(2):
                piece = wuv.at[origin(way, hop + 1), core * 2 + k]
                index = (way * 4 + hop) * 2 + k
                pair[way, hop, k] = remote(piece, piece, pair_send, pair_recv, index, sibling)

    attend_groups(0, 1)
    pl.semaphore_wait(barrier, len(peers))
    uv_load.wait()
    ring_send_hop(0, 0)
    ring_send_hop(1, 0)
    attend_groups(1, 6)
    ring_step(0)
    attend_groups(6, 8)

    order = (0, 1, -1, 2, -2, 3, -3, 4)
    moved = {}
    for n, offset in enumerate(order):
        to_z = at_z(offset * sign)
        for step in range(NX):
            to_x = at_x(step)

            @pl.loop(0, OWN, unroll=True)
            def _(j):
                head = (to_x * NZ + to_z) * OWN + j
                for k in range(LAT // LANES):
                    rows = lat32[k, pl.ds(head, SLOTS, stride=HEADS), :].astype(BF16)
                    where = pl.ds(k * LANES, LANES)
                    if step == 0:
                        lat_in[n, j, x, :, where] = rows
                    else:
                        lat_out[step - 1, n, j, :, where] = rows

            if step > 0:
                moved[n, step] = remote(
                    lat_out.at[step - 1, n], lat_in.at[n, :, x], lat_send, lat_recv,
                    (step - 1) * NZ + n, device(step, 0),
                )
        if n == 3:
            ring_step(1)

    valued = []
    for n, offset in enumerate(order):
        if n == 2:
            ring_step(2)
        if n == 4:
            ring_step(3)
        to_z = at_z(offset * sign)
        if n > 0:
            hop = abs(offset) - 1
            for k in range(2):
                pair[(1 if offset < 0 else 0), hop, k].wait_recv()
        for step in range(1, NX):
            moved[n, step].wait_recv()
        out = hv.at[z] if n == 0 else hv_out.at[n - 1]
        for j in range(OWN):
            rows = lat_in[n, j].reshape(NX * SLOTS, LAT)
            value = jnp.dot(rows, wuv[to_z, j], preferred_element_type=F32)
            out[:, pl.ds(j * VDIM, VDIM)] = value.astype(BF16)
        if n > 0:
            valued.append(remote(out, hv.at[z], hv_send, hv_recv, n - 1, device(0, offset * sign)))
    for copy in valued:
        copy.wait_recv()

    copies = {}

    def send(n, phase, way, hop):
        along_x, i, kind, _, _ = streams[n]
        axis_x = along_x == (phase == 0)
        size = NX if axis_x else NZ
        right, left = hops(size, kind)
        step = right - hop if way == 0 else hop - left
        slot = hop if way == 0 else right + hop
        if along_x:
            part = px.at[i, :, at_x(step)] if phase == 0 else px.at[i, at_z(step), x]
            land = rx1.at[i, slot] if phase == 0 else rx2.at[i, slot]
        else:
            part = pz.at[i, at_z(step)] if phase == 0 else pz.at[i, z, at_x(step)]
            land = rz1.at[i, slot] if phase == 0 else rz2.at[i, slot]
        move = 1 if way == 0 else -1
        if hop > 0:
            copies[n, phase, way, hop - 1][0].wait_recv()
            before = copies[n, phase, way, hop - 1][1]
            part[...] = (before[...].astype(F32) + part[...].astype(F32)).astype(BF16)
        copy = remote(
            part, land, send_sem, recv_sem, len(copies),
            device(move, 0) if axis_x else device(0, move),
        )
        copies[n, phase, way, hop] = (copy, land)

    def first_hops(n, phase):
        for way in (0, 1):
            send(n, phase, way, 0)

    def next_hops(n, phase, hop):
        along_x, _, kind, _, _ = streams[n]
        count = hops(NX if along_x == (phase == 0) else NZ, kind)
        for way in (0, 1):
            if hop < count[way]:
                send(n, phase, way, hop)

    def arrivals(n, phase):
        along_x, _, kind, _, _ = streams[n]
        count = hops(NX if along_x == (phase == 0) else NZ, kind)
        total = None
        for way in (0, 1):
            copy, land = copies[n, phase, way, count[way] - 1]
            copy.wait_recv()
            total = land[...].astype(F32) if total is None else total + land[...].astype(F32)
        return total

    def turn(n):
        along_x, i, _, _, _ = streams[n]
        total = arrivals(n, 0)
        mine = px.at[i, :, x] if along_x else pz.at[i, z]
        mine[...] = (mine[...].astype(F32) + total).astype(BF16)
        first_hops(n, 1)

    live = (
        lax.broadcasted_iota(jnp.int32, (SLOTS, 1), 0) < counts_ref[0]
    ).astype(F32)

    def finish(n):
        along_x, i, _, first, width = streams[n]
        total = arrivals(n, 1)
        mine = px.at[i, z, x] if along_x else pz.at[i, z, x]
        total = total + mine[...].astype(F32)
        where = pl.ds(first, width)
        hidden = (res_ref[:, where].astype(F32) + live * total).astype(BF16)
        hid_ref[:, where] = hidden
        hidden = hidden.astype(F32)
        acc[...] += jnp.sum(hidden * hidden, axis=1, keepdims=True)

    acc[...] = jnp.zeros_like(acc)
    for n, (along_x, i, _, first, width) in enumerate(streams):
        loads[n].wait()
        part = px if along_x else pz

        @pl.loop(0, width // COLS)
        def _(tile):
            off = pl.multiple_of(tile * COLS, COLS)
            out = jnp.dot(
                hv[...].reshape(NX * NZ * SLOTS, DEPTH), wo[:, pl.ds(first + off, COLS)], preferred_element_type=F32
            )
            part[i, :, :, :, pl.ds(off, COLS)] = out.astype(BF16).reshape(NZ, NX, SLOTS, COLS)

        first_hops(n, 0)

    X, Z = (0, 2, 4, 6), (1, 3, 5, 7)
    plan = [
        (next_hops, Z[0], 0, 1), (next_hops, X[0], 0, 1), (next_hops, Z[1], 0, 1),
        (next_hops, Z[2], 0, 1), (next_hops, X[1], 0, 1), (next_hops, Z[3], 0, 1),
        (next_hops, Z[0], 0, 2), (next_hops, Z[1], 0, 2), (next_hops, X[2], 0, 1),
        (next_hops, Z[2], 0, 2), (next_hops, Z[3], 0, 2),
        (turn, X[0]), (next_hops, X[3], 0, 1), (next_hops, Z[0], 0, 3), (next_hops, Z[1], 0, 3),
        (turn, X[1]), (next_hops, X[0], 1, 1),
        (next_hops, Z[2], 0, 3), (next_hops, Z[3], 0, 3),
        (next_hops, X[1], 1, 1), (next_hops, X[0], 1, 2), (turn, Z[0]), (turn, Z[1]),
        (next_hops, X[1], 1, 2), (next_hops, X[0], 1, 3), (next_hops, X[1], 1, 3),
        (turn, X[2]), (turn, Z[2]), (turn, Z[3]), (turn, X[3]),
        (next_hops, Z[0], 1, 1), (next_hops, Z[1], 1, 1),
        (next_hops, X[2], 1, 1), (next_hops, X[3], 1, 1),
        (next_hops, Z[2], 1, 1), (next_hops, Z[3], 1, 1),
        (next_hops, X[2], 1, 2), (next_hops, X[3], 1, 2),
        (finish, X[0]), (finish, X[1]),
        (next_hops, X[2], 1, 3), (next_hops, X[3], 1, 3),
        (finish, Z[0]), (finish, Z[1]), (finish, Z[2]), (finish, Z[3]),
        (finish, X[2]), (finish, X[3]),
    ]
    for act, *rest in plan:
        act(*rest)

    inv = lax.rsqrt(acc[...] * (1.0 / WIDTH) + norm_eps)
    mlp_ref[...] = (hid_ref[...].astype(F32) * inv * gain_ref[...].astype(F32)).astype(BF16)
    for copy in started:
        copy.wait_send()


def body(
    q_latent, q_rope, cache_latent, rope_keys, lengths, counts, w_uv, w_o, residual, norm_gain
):
    vmem = pl.BlockSpec(memory_space=pltpu.VMEM)
    smem = pl.BlockSpec(memory_space=pltpu.SMEM)
    hbm = pl.BlockSpec(memory_space=pl.ANY)
    dma = pltpu.SemaphoreType.DMA
    rows = NX * NZ * SLOTS
    outs = pl.pallas_call(
        decode_kernel,
        out_shape=[jax.ShapeDtypeStruct((SLOTS, WIDTH), BF16)] * 2,
        in_specs=[hbm] * 6 + [smem] * 2 + [vmem] * 2,
        out_specs=[vmem, vmem],
        scratch_shapes=[
            pltpu.VMEM((SLOTS, HEADS, LAT), BF16),
            pltpu.VMEM((SLOTS, ROPE, HEADS), BF16),
            pltpu.VMEM((SLOTS, CTX, LAT), BF16),
            pltpu.VMEM((SLOTS, ROPE, CTX), BF16),
            pltpu.VMEM((LAT // LANES, SLOTS * HEADS, LANES), F32),
            pltpu.VMEM((NX - 1, NZ, OWN, SLOTS, LAT), BF16),
            pltpu.VMEM((NZ, OWN, NX, SLOTS, LAT), BF16),
            pltpu.VMEM((NZ, OWN, LAT, VDIM), BF16),
            pltpu.VMEM((NZ - 1, NX * SLOTS, DEPTH), BF16),
            pltpu.VMEM((NZ, NX * SLOTS, DEPTH), BF16),
            pltpu.VMEM((DEPTH, WIDTH), BF16),
            pltpu.VMEM((4, NZ, NX, SLOTS, XW), BF16),
            pltpu.VMEM((4, NZ, NX, SLOTS, ZW), BF16),
            pltpu.VMEM((4, 3, NZ, SLOTS, XW), BF16),
            pltpu.VMEM((4, 7, SLOTS, XW), BF16),
            pltpu.VMEM((4, 7, NX, SLOTS, ZW), BF16),
            pltpu.VMEM((4, 3, SLOTS, ZW), BF16),
            pltpu.VMEM((SLOTS, 1), F32),
            dma((4, SLOTS // GROUP)), dma, dma((8,)),
            dma((16,)), dma((16,)), dma((16,)), dma((16,)),
            dma((24,)), dma((24,)), dma((7,)), dma((7,)), dma((80,)), dma((80,)),
        ],
        compiler_params=pltpu.CompilerParams(
            collective_id=0, has_side_effects=True, vmem_limit_bytes=56 * 1024 * 1024
        ),
        cost_estimate=pl.CostEstimate(
            flops=2 * rows * DEPTH * WIDTH, bytes_accessed=20 * 1024 * 1024, transcendentals=0
        ),
    )(
        q_latent, q_rope, cache_latent, rope_keys, w_uv, w_o, lengths, counts, residual,
        norm_gain.reshape(1, WIDTH),
    )
    return tuple(outs)


def solution(mesh):
    in_specs = (
        P(("grp", "dp"), None, None),
        P(("grp", "dp"), None, None),
        P(("grp", "dp"), None, None),
        P(("grp", "dp"), None, None),
        P(("grp", "dp")),
        P(("grp", "dp")),
        P("dp", None, None),
        P("dp", None),
        P(("grp", "dp"), None),
        P(),
    )
    out_specs = (P(("grp", "dp"), None), P(("grp", "dp"), None))
    return jax.shard_map(body, mesh=mesh, in_specs=in_specs, out_specs=out_specs, check_vma=False)
```

```python
import jax
import jax.numpy as jnp
from jax import lax
from jax.experimental import pallas as pl
from jax.experimental.pallas import tpu as pltpu
from jax.sharding import PartitionSpec as P

score_scale = 192.0 ** (-0.5)
log2_e = 1.4426950408889634
norm_eps = 1e-06

NX, NZ = 4, 8
SLOTS = 16
HEADS, LAT, VDIM, ROPE, CTX = 128, 512, 128, 64, 512
OWN = 4
WIDTH = 7168
DEPTH = OWN * VDIM
COLS = 256
GROUP = 2
LANES = 128
XW, ZW = 1024, 768
MESH = pl.DeviceIdType.MESH
F32, BF16 = jnp.float32, jnp.bfloat16


def hops(size, kind):
    long, short = size // 2, size // 2 - 1
    return (long, short) if kind == 0 else (short, long)


def decode_kernel(
    q_hbm, qr_hbm, cache_hbm, rope_hbm, wuv_hbm, wo_hbm, lengths_ref, counts_ref, res_ref, gain_ref,
    hid_ref, mlp_ref,
    q_ref, qr_ref, cache_ref, rope_ref, lat32, lat_out, lat_in, wuv, hv_out, hv,
    wo, px, pz, rx1, rx2, rz1, rz2, acc,
    slot_sem, uv_sem, load_sem,
    ring_send, ring_recv, pair_send, pair_recv, lat_send, lat_recv, hv_send, hv_recv, send_sem, recv_sem,
):
    dp, grp = lax.axis_index("dp"), lax.axis_index("grp")
    x, z = dp // NZ, dp % NZ
    core = grp % 2
    sign = 1 - 2 * core
    sibling = (dp, grp + sign)

    def at_x(step):
        return (x + step + NX) % NX

    def at_z(step):
        return (z + step + NZ) % NZ

    def device(dx, dz):
        return (at_x(dx) * NZ + at_z(dz), grp)

    started = []

    def remote(src, dst, sends, recvs, index, target):
        copy = pltpu.make_async_remote_copy(
            src_ref=src, dst_ref=dst, send_sem=sends.at[index], recv_sem=recvs.at[index],
            device_id=target, device_id_type=MESH,
        )
        copy.start()
        started.append(copy)
        return copy

    barrier = pltpu.get_barrier_semaphore()
    peers = [device(d, 0) for d in range(1, NX)] + [device(0, d) for d in range(1, NZ)] + [sibling]
    for peer in peers:
        pl.semaphore_signal(barrier, inc=1, device_id=peer, device_id_type=MESH)

    uv_loads = [
        pltpu.make_async_copy(
            wuv_hbm.at[j], wuv.at[z, j // 2, :, pl.ds(j % 2 * VDIM, VDIM)], uv_sem.at[j]
        )
        for j in range(OWN)
    ]
    for load in uv_loads:
        load.start()

    def slot_loads(group):
        where = pl.ds(group * GROUP, GROUP)
        return [
            pltpu.make_async_copy(hbm.at[where], vmem.at[where], slot_sem.at[n, group])
            for n, (hbm, vmem) in enumerate(
                ((q_hbm, q_ref), (cache_hbm, cache_ref), (qr_hbm, qr_ref), (rope_hbm, rope_ref))
            )
        ]

    for group in range(SLOTS // GROUP):
        for load in slot_loads(group):
            load.start()

    streams = []
    for i in range(4):
        streams.append((True, i, i % 2, i * XW, XW))
        streams.append((False, i, i % 2, 4 * XW + i * ZW, ZW))
    loads = []
    for n, (_, _, _, first, width) in enumerate(streams):
        load = pltpu.make_async_copy(
            wo_hbm.at[:, pl.ds(first, width)], wo.at[:, pl.ds(first, width)], load_sem.at[n]
        )
        load.start()
        loads.append(load)

    position = lax.broadcasted_iota(jnp.int32, (1, CTX), 1)

    def attend(slot):
        scores = lax.dot_general(
            q_ref[slot], cache_ref[slot], (((1,), (1,)), ((), ())), preferred_element_type=F32
        )
        scores += lax.dot_general(
            qr_ref[slot], rope_ref[slot], (((0,), (0,)), ((), ())), preferred_element_type=F32
        )
        scores = jnp.where(position < lengths_ref[slot], scores, -1e30)
        top = jnp.max(scores, axis=1, keepdims=True)
        expos = jnp.exp2((scores - top) * (score_scale * log2_e))
        probs = (expos * (1.0 / jnp.sum(expos, axis=1, keepdims=True))).astype(BF16)
        rows = pl.ds(pl.multiple_of(slot * HEADS, HEADS), HEADS)
        latents = jnp.dot(probs, cache_ref[slot], preferred_element_type=F32)
        for k in range(LAT // LANES):
            lat32[k, rows, :] = latents[:, k * LANES : (k + 1) * LANES]

    def attend_groups(first, last):
        @pl.loop(first, last)
        def _(group):
            for load in slot_loads(group):
                load.wait()
            for j in range(GROUP):
                attend(group * GROUP + j)

    ring_hops = (NZ // 2, NZ // 2 - 1)
    ring, pair = {}, {}

    def uv_piece(way, hop, k):
        origin = at_z(hop * (-sign if way == 0 else sign))
        return wuv.at[origin, core, pl.ds(k * (LAT // 2), LAT // 2)]

    def ring_hop(way, hop, k):
        to = (x * NZ + at_z(sign if way == 0 else -sign), grp)
        piece = uv_piece(way, hop, k)
        index = (way * 4 + hop) * 2 + k
        ring[way, hop, k] = remote(piece, piece, ring_send, ring_recv, index, to)

    def ring_step(hop, k):
        for way in (0, 1):
            if hop >= ring_hops[way]:
                continue
            ring[way, hop, k].wait_recv()
            if hop + 1 < ring_hops[way]:
                ring_hop(way, hop + 1, k)
            piece = uv_piece(way, hop + 1, k)
            index = (way * 4 + hop) * 2 + k
            pair[way, hop, k] = remote(piece, piece, pair_send, pair_recv, index, sibling)

    order = ((0, 1), (-1, 2), (-2, 3), (-3, 4))
    moved = {}

    def move_half(half):
        for m, offsets in enumerate(order):
            for step in (1, 3, 2, 0):
                to_x = at_x(step)
                for i, offset in enumerate(offsets):
                    first = (to_x * NZ + at_z(offset * sign)) * OWN
                    for p in range(OWN // 2):
                        for k in range(LAT // LANES):
                            rows = jnp.concatenate(
                                [
                                    lat32[k, pl.ds(half * 8 * HEADS + first + 2 * p + j, 8, stride=HEADS), :]
                                    for j in range(2)
                                ],
                                axis=0,
                            ).astype(BF16)
                            where = pl.ds(k * LANES, LANES)
                            if step == 0:
                                lat_in[half, m, x, i, p, :, where] = rows
                            else:
                                lat_out[half, step - 1, m, i, p, :, where] = rows
                if step > 0:
                    moved[half, m, step] = remote(
                        lat_out.at[half, step - 1, m], lat_in.at[half, m, x], lat_send, lat_recv,
                        (half * 3 + step - 1) * 4 + m, device(step, 0),
                    )

    valued = []

    def head_values(m):
        for half in range(2):
            for step in range(1, NX):
                moved[half, m, step].wait_recv()
        for i, offset in enumerate(order[m]):
            n = 2 * m + i
            to_z = at_z(offset * sign)
            if n > 0:
                for k in range(2):
                    pair[(1 if offset < 0 else 0), abs(offset) - 1, k].wait_recv()
            for p in range(OWN // 2):
                rows = lat_in[:, m, :, i, p].reshape(2 * NX * SLOTS, LAT)
                value = jnp.dot(rows, wuv[to_z, p], preferred_element_type=F32)
                value = value.reshape(2, NX, 2, 8, 2 * VDIM)
                for row in range(NX):
                    halves = [
                        jnp.concatenate([value[h, row, 0, :, :VDIM], value[h, row, 1, :, VDIM:]], axis=1)
                        for h in range(2)
                    ]
                    rows = jnp.concatenate(halves, axis=0).astype(BF16)
                    at = (pl.ds(row * SLOTS, SLOTS), pl.ds(p * 2 * VDIM, 2 * VDIM))
                    if n == 0:
                        hv[z, at[0], at[1]] = rows
                    else:
                        hv_out[n - 1, at[0], at[1]] = rows
            if n > 0:
                valued.append(
                    remote(hv_out.at[n - 1], hv.at[z], hv_send, hv_recv, n - 1, device(0, offset * sign))
                )

    attend_groups(0, 1)
    pl.semaphore_wait(barrier, len(peers))
    for load in uv_loads:
        load.wait()
    for k in range(2):
        ring_hop(0, 0, k)
        ring_hop(1, 0, k)
    attend_groups(1, 4)
    move_half(0)
    ring_step(0, 0)
    attend_groups(4, 6)
    ring_step(0, 1)
    attend_groups(6, 8)
    ring_step(1, 0)
    move_half(1)
    ring_step(1, 1)
    ring_step(2, 0)
    ring_step(2, 1)
    head_values(0)
    ring_step(3, 0)
    head_values(1)
    ring_step(3, 1)
    head_values(2)
    head_values(3)
    for copy in valued:
        copy.wait_recv()

    copies = {}

    def send(n, phase, way, hop):
        along_x, i, kind, _, _ = streams[n]
        axis_x = along_x == (phase == 0)
        size = NX if axis_x else NZ
        right, left = hops(size, kind)
        step = right - hop if way == 0 else hop - left
        slot = hop if way == 0 else right + hop
        if along_x:
            part = px.at[i, :, at_x(step)] if phase == 0 else px.at[i, at_z(step), x]
            land = rx1.at[i, slot] if phase == 0 else rx2.at[i, slot]
        else:
            part = pz.at[i, at_z(step)] if phase == 0 else pz.at[i, z, at_x(step)]
            land = rz1.at[i, slot] if phase == 0 else rz2.at[i, slot]
        move = 1 if way == 0 else -1
        if hop > 0:
            copies[n, phase, way, hop - 1][0].wait_recv()
            before = copies[n, phase, way, hop - 1][1]
            part[...] = (before[...].astype(F32) + part[...].astype(F32)).astype(BF16)
        copy = remote(
            part, land, send_sem, recv_sem, len(copies),
            device(move, 0) if axis_x else device(0, move),
        )
        copies[n, phase, way, hop] = (copy, land)

    def first_hops(n, phase):
        for way in (0, 1):
            send(n, phase, way, 0)

    def arrivals(n, phase):
        along_x, _, kind, _, _ = streams[n]
        count = hops(NX if along_x == (phase == 0) else NZ, kind)
        total = None
        for way in (0, 1):
            copy, land = copies[n, phase, way, count[way] - 1]
            copy.wait_recv()
            total = land[...].astype(F32) if total is None else total + land[...].astype(F32)
        return total

    def turn(n):
        along_x, i, _, _, _ = streams[n]
        total = arrivals(n, 0)
        mine = px.at[i, :, x] if along_x else pz.at[i, z]
        mine[...] = (mine[...].astype(F32) + total).astype(BF16)
        first_hops(n, 1)

    live = (
        lax.broadcasted_iota(jnp.int32, (SLOTS, 1), 0) < counts_ref[0]
    ).astype(F32)

    def finish(n):
        along_x, i, _, first, width = streams[n]
        total = arrivals(n, 1)
        mine = px.at[i, z, x] if along_x else pz.at[i, z, x]
        total = total + mine[...].astype(F32)
        where = pl.ds(first, width)
        hidden = (res_ref[:, where].astype(F32) + live * total).astype(BF16)
        hid_ref[:, where] = hidden
        hidden = hidden.astype(F32)
        acc[...] += jnp.sum(hidden * hidden, axis=1, keepdims=True)

    def multiply(n):
        along_x, i, _, first, width = streams[n]
        loads[n].wait()
        part = px if along_x else pz

        @pl.loop(0, width // COLS)
        def _(tile):
            off = pl.multiple_of(tile * COLS, COLS)
            out = jnp.dot(
                hv[...].reshape(NX * NZ * SLOTS, DEPTH), wo[:, pl.ds(first + off, COLS)],
                preferred_element_type=F32,
            )
            part[i, :, :, :, pl.ds(off, COLS)] = out.astype(BF16).reshape(NZ, NX, SLOTS, COLS)

        first_hops(n, 0)

    acc[...] = jnp.zeros_like(acc)
    for n in range(8):
        multiply(n)
    for step in (
        (1, 0, 0, 1), (1, 0, 1, 1), (3, 0, 0, 1), (3, 0, 1, 1), (0, 0, 0, 1), (5, 0, 0, 1),
        (5, 0, 1, 1), (7, 0, 0, 1), (7, 0, 1, 1), (2, 0, 1, 1), (1, 0, 0, 2), (1, 0, 1, 2),
        (3, 0, 0, 2), (3, 0, 1, 2), (5, 0, 0, 2), (5, 0, 1, 2), (4, 0, 0, 1), (7, 0, 0, 2),
        (7, 0, 1, 2), (1, 0, 0, 3), (3, 0, 1, 3), (6, 0, 1, 1), (5, 0, 0, 3), (7, 0, 1, 3),
        (turn, 0), (turn, 1), (turn, 2), (turn, 3), (turn, 5), (turn, 7),
        (0, 1, 0, 1), (0, 1, 1, 1), (2, 1, 0, 1), (2, 1, 1, 1), (turn, 4), (turn, 6),
        (0, 1, 0, 2), (0, 1, 1, 2), (2, 1, 0, 2), (2, 1, 1, 2), (1, 1, 0, 1), (3, 1, 1, 1),
        (5, 1, 0, 1), (7, 1, 1, 1), (4, 1, 0, 1), (4, 1, 1, 1), (6, 1, 0, 1), (6, 1, 1, 1),
        (finish, 1), (finish, 3), (0, 1, 0, 3), (finish, 5), (finish, 7), (2, 1, 1, 3),
        (4, 1, 0, 2), (4, 1, 1, 2), (6, 1, 0, 2), (6, 1, 1, 2), (finish, 0), (finish, 2),
        (4, 1, 0, 3), (6, 1, 1, 3), (finish, 4), (finish, 6),
    ):
        if len(step) == 4:
            send(*step)
        else:
            step[0](step[1])

    inv = lax.rsqrt(acc[...] * (1.0 / WIDTH) + norm_eps)
    gain = gain_ref[...].astype(F32)
    for k in range(WIDTH // LANES):
        where = pl.ds(k * LANES, LANES)
        mlp_ref[:, where] = (hid_ref[:, where].astype(F32) * inv * gain[k : k + 1, :]).astype(BF16)
    for copy in started:
        copy.wait_send()


def body(
    q_latent, q_rope, cache_latent, rope_keys, lengths, counts, w_uv, w_o, residual, norm_gain
):
    vmem = pl.BlockSpec(memory_space=pltpu.VMEM)
    smem = pl.BlockSpec(memory_space=pltpu.SMEM)
    hbm = pl.BlockSpec(memory_space=pl.ANY)
    dma = pltpu.SemaphoreType.DMA
    rows = NX * NZ * SLOTS
    outs = pl.pallas_call(
        decode_kernel,
        out_shape=[jax.ShapeDtypeStruct((SLOTS, WIDTH), BF16)] * 2,
        in_specs=[hbm] * 6 + [smem] * 2 + [vmem] * 2,
        out_specs=[vmem, vmem],
        scratch_shapes=[
            pltpu.VMEM((SLOTS, HEADS, LAT), BF16),
            pltpu.VMEM((SLOTS, ROPE, HEADS), BF16),
            pltpu.VMEM((SLOTS, CTX, LAT), BF16),
            pltpu.VMEM((SLOTS, ROPE, CTX), BF16),
            pltpu.VMEM((LAT // LANES, SLOTS * HEADS, LANES), F32),
            pltpu.VMEM((2, NX - 1, 4, 2, OWN // 2, SLOTS, LAT), BF16),
            pltpu.VMEM((2, 4, NX, 2, OWN // 2, SLOTS, LAT), BF16),
            pltpu.VMEM((NZ, OWN // 2, LAT, 2 * VDIM), BF16),
            pltpu.VMEM((NZ - 1, NX * SLOTS, DEPTH), BF16),
            pltpu.VMEM((NZ, NX * SLOTS, DEPTH), BF16),
            pltpu.VMEM((DEPTH, WIDTH), BF16),
            pltpu.VMEM((4, NZ, NX, SLOTS, XW), BF16),
            pltpu.VMEM((4, NZ, NX, SLOTS, ZW), BF16),
            pltpu.VMEM((4, 3, NZ, SLOTS, XW), BF16),
            pltpu.VMEM((4, 7, SLOTS, XW), BF16),
            pltpu.VMEM((4, 7, NX, SLOTS, ZW), BF16),
            pltpu.VMEM((4, 3, SLOTS, ZW), BF16),
            pltpu.VMEM((SLOTS, 1), F32),
            dma((4, SLOTS // GROUP)), dma((OWN,)), dma((8,)),
            dma((16,)), dma((16,)), dma((16,)), dma((16,)),
            dma((24,)), dma((24,)), dma((7,)), dma((7,)), dma((80,)), dma((80,)),
        ],
        compiler_params=pltpu.CompilerParams(
            collective_id=0, has_side_effects=True, vmem_limit_bytes=56 * 1024 * 1024
        ),
        cost_estimate=pl.CostEstimate(
            flops=2 * rows * DEPTH * WIDTH, bytes_accessed=20 * 1024 * 1024, transcendentals=0
        ),
    )(
        q_latent, q_rope, cache_latent, rope_keys, w_uv, w_o, lengths, counts, residual,
        norm_gain.reshape(WIDTH // LANES, LANES),
    )
    return tuple(outs)


def solution(mesh):
    in_specs = (
        P(("grp", "dp"), None, None),
        P(("grp", "dp"), None, None),
        P(("grp", "dp"), None, None),
        P(("grp", "dp"), None, None),
        P(("grp", "dp")),
        P(("grp", "dp")),
        P("dp", None, None),
        P("dp", None),
        P(("grp", "dp"), None),
        P(),
    )
    out_specs = (P(("grp", "dp"), None), P(("grp", "dp"), None))
    return jax.shard_map(body, mesh=mesh, in_specs=in_specs, out_specs=out_specs, check_vma=False)
```

```python
import jax
import jax.numpy as jnp
from jax import lax
from jax.experimental import pallas as pl
from jax.experimental.pallas import tpu as pltpu
from jax.sharding import PartitionSpec as P

score_scale = 192.0 ** (-0.5)
log2_e = 1.4426950408889634
norm_eps = 1e-06

NX, NY, NZ = 4, 4, 8
SLOTS = 16
HEADS, LAT, VDIM, ROPE, CTX = 128, 512, 128, 64, 512
OWN = 4
WIDTH = 7168
DEPTH = OWN * VDIM
COLS = 256
GROUP = 4
LANES = 128
XW, ZW = 1024, 768
MESH = pl.DeviceIdType.MESH
F32, BF16 = jnp.float32, jnp.bfloat16


def hops(size, kind):
    long, short = size // 2, size // 2 - 1
    return (long, short) if kind == 0 else (short, long)


def decode_kernel(
    q_hbm, qr_hbm, cache_hbm, rope_hbm, wuv_hbm, wo_hbm, res_hbm, gain_hbm, lengths_ref, counts_ref,
    hid_ref, mlp_ref,
    res_ref, gain_ref, q_ref, qr_ref, cache_ref, rope_ref, lat32, lat_out, lat_in, wuv, hv_out, hv,
    wo, px, pz, rx1, rx2, rz1, rz2, acc,
    row_sem, slot_sem, uv_sem, load_sem,
    ring_send, ring_recv, cross_send, cross_recv, pair_send, pair_recv, lat_send, lat_recv, hv_send, hv_recv, send_sem, recv_sem,
):
    dp, grp = lax.axis_index("dp"), lax.axis_index("grp")
    x, z = dp // NZ, dp % NZ
    y, core = grp // 2, grp % 2
    sign = 1 - 2 * core
    sibling = (dp, grp + sign)
    y_pair = y % 2

    def plane(step):
        return (dp, (y + step + NY) % NY * 2 + core)

    def at_x(step):
        return (x + step + NX) % NX

    def at_z(step):
        return (z + step + NZ) % NZ

    def device(dx, dz):
        return (at_x(dx) * NZ + at_z(dz), grp)

    started = []

    def remote(src, dst, sends, recvs, index, target):
        copy = pltpu.make_async_remote_copy(
            src_ref=src, dst_ref=dst, send_sem=sends.at[index], recv_sem=recvs.at[index],
            device_id=target, device_id_type=MESH,
        )
        copy.start()
        started.append(copy)
        return copy

    barrier = pltpu.get_barrier_semaphore()
    peers = [device(d, 0) for d in range(1, NX)] + [device(0, d) for d in range(1, NZ)]
    peers += [sibling, plane(1), plane(-1)]
    for peer in peers:
        pl.semaphore_signal(barrier, inc=1, device_id=peer, device_id_type=MESH)

    def slot_loads(group):
        where = pl.ds(group * GROUP, GROUP)
        return [
            pltpu.make_async_copy(hbm.at[where], vmem.at[where], slot_sem.at[n, group])
            for n, (hbm, vmem) in enumerate(
                ((q_hbm, q_ref), (cache_hbm, cache_ref), (qr_hbm, qr_ref), (rope_hbm, rope_ref))
            )
        ]

    for load in slot_loads(0):
        load.start()
    uv_loads = [
        pltpu.make_async_copy(
            wuv_hbm.at[j], wuv.at[z, j // 2, :, pl.ds(j % 2 * VDIM, VDIM)], uv_sem.at[j]
        )
        for j in range(OWN)
    ]
    for load in uv_loads:
        load.start()
    for group in range(1, SLOTS // GROUP):
        for load in slot_loads(group):
            load.start()
    row_loads = [
        pltpu.make_async_copy(res_hbm, res_ref, row_sem.at[0]),
        pltpu.make_async_copy(gain_hbm, gain_ref, row_sem.at[1]),
    ]
    for load in row_loads:
        load.start()

    streams = []
    for i in range(4):
        streams.append((True, i, i % 2, i * XW, XW))
        streams.append((False, i, i % 2, 4 * XW + i * ZW, ZW))
    loads = []
    for n, (_, _, _, first, width) in enumerate(streams):
        load = pltpu.make_async_copy(
            wo_hbm.at[:, pl.ds(first, width)], wo.at[:, pl.ds(first, width)], load_sem.at[n]
        )
        load.start()
        loads.append(load)

    position = lax.broadcasted_iota(jnp.int32, (1, CTX), 1)

    def score(slot):
        scores = lax.dot_general(
            q_ref[slot], cache_ref[slot], (((1,), (1,)), ((), ())), preferred_element_type=F32
        )
        scores += lax.dot_general(
            qr_ref[slot], rope_ref[slot], (((0,), (0,)), ((), ())), preferred_element_type=F32
        )
        return jnp.where(position < lengths_ref[slot], scores, -1e30)

    def soften(scores):
        top = jnp.max(scores, axis=1, keepdims=True)
        expos = jnp.exp2((scores - top) * (score_scale * log2_e))
        return (expos * (1.0 / jnp.sum(expos, axis=1, keepdims=True))).astype(BF16)

    def gather(slot, probs):
        rows = pl.ds(pl.multiple_of(slot * HEADS, HEADS), HEADS)
        latents = jnp.dot(probs, cache_ref[slot], preferred_element_type=F32)
        for k in range(LAT // LANES):
            lat32[k, rows, :] = latents[:, k * LANES : (k + 1) * LANES]

    def attend_groups(first, last):
        @pl.loop(first, last)
        def _(group):
            for load in slot_loads(group):
                load.wait()
            first = group * GROUP
            scores = [score(first)]
            for j in range(GROUP):
                if j + 1 < GROUP:
                    scores.append(score(first + j + 1))
                gather(first + j, soften(scores[j]))

    ring_hops = (NZ // 2, NZ // 2 - 1)
    ring, pair, cross, cross_pair = {}, {}, {}, {}

    def uv_piece(way, hop, which):
        origin = at_z(hop * (-sign if way == 0 else sign))
        return wuv.at[origin, which, pl.ds(pl.multiple_of(core * (LAT // 2), LAT // 2), LAT // 2)]

    def ring_hop(way, hop):
        to = (x * NZ + at_z(sign if way == 0 else -sign), grp)
        piece = uv_piece(way, hop, y_pair)
        ring[way, hop] = remote(piece, piece, ring_send, ring_recv, way * 4 + hop, to)

    def ring_step(hop):
        for way in (0, 1):
            if hop >= ring_hops[way]:
                continue
            ring[way, hop].wait_recv()
            if hop + 1 < ring_hops[way]:
                ring_hop(way, hop + 1)
            piece = uv_piece(way, hop + 1, y_pair)
            index = way * 4 + hop
            cross[way, hop] = remote(piece, piece, cross_send, cross_recv, index, plane(sign))
            pair[way, hop] = remote(piece, piece, pair_send, pair_recv, index, sibling)

    def cross_step(hop):
        for way in (0, 1):
            if hop >= ring_hops[way]:
                continue
            cross[way, hop].wait_recv()
            piece = uv_piece(way, hop + 1, 1 - y_pair)
            index = 8 + way * 4 + hop
            cross_pair[way, hop] = remote(piece, piece, pair_send, pair_recv, index, sibling)

    order = ((3, -3), (4, 2), (-2, 1), (-1, 0))
    moved = {}

    def move_half(half):
        for m, offsets in enumerate(order):
            for step in (1, 3, 2, 0):
                to_x = at_x(step)
                for i, offset in enumerate(offsets):
                    first = (to_x * NZ + at_z(offset * sign)) * OWN
                    for p in range(OWN // 2):
                        for k in range(LAT // LANES):
                            rows = jnp.concatenate(
                                [
                                    lat32[k, pl.ds(half * 8 * HEADS + first + 2 * p + j, 8, stride=HEADS), :]
                                    for j in range(2)
                                ],
                                axis=0,
                            ).astype(BF16)
                            where = pl.ds(k * LANES, LANES)
                            if step == 0:
                                lat_in[half, m, x, i, p, :, where] = rows
                            else:
                                lat_out[half, step - 1, m, i, p, :, where] = rows
                if step > 0:
                    moved[half, m, step] = remote(
                        lat_out.at[half, step - 1, m], lat_in.at[half, m, x], lat_send, lat_recv,
                        (half * 3 + step - 1) * 4 + m, device(step, 0),
                    )

    valued = []

    def head_values(m):
        for half in range(2):
            for step in range(1, NX):
                moved[half, m, step].wait_recv()
        for i, offset in enumerate(order[m]):
            n = 2 * m + i
            to_z = at_z(offset * sign)
            if offset != 0:
                came = (1 if offset < 0 else 0, abs(offset) - 1)
                pair[came].wait_recv()
                cross_pair[came].wait_recv()
            for p in range(OWN // 2):
                rows = lat_in[:, m, :, i, p].reshape(2 * NX * SLOTS, LAT)
                value = jnp.dot(rows, wuv[to_z, p], preferred_element_type=F32)
                value = value.reshape(2, NX, 2, 8, 2 * VDIM)
                for row in range(NX):
                    halves = [
                        jnp.concatenate([value[h, row, 0, :, :VDIM], value[h, row, 1, :, VDIM:]], axis=1)
                        for h in range(2)
                    ]
                    rows = jnp.concatenate(halves, axis=0).astype(BF16)
                    at = (pl.ds(row * SLOTS, SLOTS), pl.ds(p * 2 * VDIM, 2 * VDIM))
                    if offset == 0:
                        hv[z, at[0], at[1]] = rows
                    else:
                        hv_out[n, at[0], at[1]] = rows
            if offset != 0:
                valued.append(
                    remote(hv_out.at[n], hv.at[z], hv_send, hv_recv, n, device(0, offset * sign))
                )

    attend_groups(0, 1)
    pl.semaphore_wait(barrier, len(peers))
    for load in uv_loads:
        load.wait()
    ring_hop(0, 0)
    ring_hop(1, 0)
    attend_groups(1, 2)
    move_half(0)
    attend_groups(2, 3)
    ring_step(0)
    attend_groups(3, 4)
    move_half(1)
    ring_step(1)
    cross_step(0)
    ring_step(2)
    cross_step(1)
    cross_step(2)
    ring_step(3)
    head_values(0)
    cross_step(3)
    for m in range(1, 4):
        head_values(m)
    for copy in valued:
        copy.wait_recv()

    copies = {}

    def send(n, phase, way, hop):
        along_x, i, kind, _, _ = streams[n]
        axis_x = along_x == (phase == 0)
        size = NX if axis_x else NZ
        right, left = hops(size, kind)
        step = right - hop if way == 0 else hop - left
        slot = hop if way == 0 else right + hop
        if along_x:
            part = px.at[i, :, at_x(step)] if phase == 0 else px.at[i, at_z(step), x]
            land = rx1.at[i, slot] if phase == 0 else rx2.at[i, slot]
        else:
            part = pz.at[i, at_z(step)] if phase == 0 else pz.at[i, z, at_x(step)]
            land = rz1.at[i, slot] if phase == 0 else rz2.at[i, slot]
        move = 1 if way == 0 else -1
        if hop > 0:
            copies[n, phase, way, hop - 1][0].wait_recv()
            before = copies[n, phase, way, hop - 1][1]
            part[...] = (before[...].astype(F32) + part[...].astype(F32)).astype(BF16)
        copy = remote(
            part, land, send_sem, recv_sem, len(copies),
            device(move, 0) if axis_x else device(0, move),
        )
        copies[n, phase, way, hop] = (copy, land)

    def first_hops(n, phase):
        for way in (0, 1):
            send(n, phase, way, 0)

    def arrivals(n, phase):
        along_x, _, kind, _, _ = streams[n]
        count = hops(NX if along_x == (phase == 0) else NZ, kind)
        total = None
        for way in (0, 1):
            copy, land = copies[n, phase, way, count[way] - 1]
            copy.wait_recv()
            total = land[...].astype(F32) if total is None else total + land[...].astype(F32)
        return total

    def turn(n):
        along_x, i, _, _, _ = streams[n]
        total = arrivals(n, 0)
        mine = px.at[i, :, x] if along_x else pz.at[i, z]
        mine[...] = (mine[...].astype(F32) + total).astype(BF16)
        first_hops(n, 1)

    live = (
        lax.broadcasted_iota(jnp.int32, (SLOTS, 1), 0) < counts_ref[0]
    ).astype(F32)

    def finish(n):
        along_x, i, _, first, width = streams[n]
        total = arrivals(n, 1)
        mine = px.at[i, z, x] if along_x else pz.at[i, z, x]
        total = total + mine[...].astype(F32)
        where = pl.ds(first, width)
        hidden = (res_ref[:, where].astype(F32) + live * total).astype(BF16)
        hid_ref[:, where] = hidden
        hidden = hidden.astype(F32)
        acc[...] += jnp.sum(hidden * hidden, axis=1, keepdims=True)

    def multiply(n):
        along_x, i, _, first, width = streams[n]
        loads[n].wait()
        part = px if along_x else pz

        @pl.loop(0, width // COLS)
        def _(tile):
            off = pl.multiple_of(tile * COLS, COLS)
            out = jnp.dot(
                hv[...].reshape(NX * NZ * SLOTS, DEPTH), wo[:, pl.ds(first + off, COLS)],
                preferred_element_type=F32,
            )
            part[i, :, :, :, pl.ds(off, COLS)] = out.astype(BF16).reshape(NZ, NX, SLOTS, COLS)

        first_hops(n, 0)

    acc[...] = jnp.zeros_like(acc)
    for load in row_loads:
        load.wait()
    for n in range(8):
        multiply(n)
    for step in (
        (1, 0, 0, 1), (1, 0, 1, 1), (3, 0, 0, 1), (3, 0, 1, 1), (0, 0, 0, 1), (5, 0, 0, 1),
        (5, 0, 1, 1), (7, 0, 0, 1), (7, 0, 1, 1), (2, 0, 1, 1), (1, 0, 0, 2), (1, 0, 1, 2),
        (3, 0, 0, 2), (3, 0, 1, 2), (5, 0, 0, 2), (5, 0, 1, 2), (4, 0, 0, 1), (7, 0, 0, 2),
        (7, 0, 1, 2), (1, 0, 0, 3), (3, 0, 1, 3), (6, 0, 1, 1), (5, 0, 0, 3), (7, 0, 1, 3),
        (turn, 0), (turn, 1), (turn, 2), (turn, 3), (turn, 5), (turn, 7),
        (0, 1, 0, 1), (0, 1, 1, 1), (2, 1, 0, 1), (2, 1, 1, 1), (turn, 4), (turn, 6),
        (0, 1, 0, 2), (0, 1, 1, 2), (2, 1, 0, 2), (2, 1, 1, 2), (1, 1, 0, 1), (3, 1, 1, 1),
        (5, 1, 0, 1), (7, 1, 1, 1), (4, 1, 0, 1), (4, 1, 1, 1), (6, 1, 0, 1), (6, 1, 1, 1),
        (finish, 1), (finish, 3), (0, 1, 0, 3), (finish, 5), (finish, 7), (2, 1, 1, 3),
        (4, 1, 0, 2), (4, 1, 1, 2), (6, 1, 0, 2), (6, 1, 1, 2), (finish, 0), (finish, 2),
        (4, 1, 0, 3), (6, 1, 1, 3), (finish, 4), (finish, 6),
    ):
        if len(step) == 4:
            send(*step)
        else:
            step[0](step[1])

    inv = lax.rsqrt(acc[...] * (1.0 / WIDTH) + norm_eps)
    gain = gain_ref[...].astype(F32)
    for k in range(WIDTH // LANES):
        where = pl.ds(k * LANES, LANES)
        mlp_ref[:, where] = (hid_ref[:, where].astype(F32) * inv * gain[k : k + 1, :]).astype(BF16)
    for copy in started:
        copy.wait_send()


def body(
    q_latent, q_rope, cache_latent, rope_keys, lengths, counts, w_uv, w_o, residual, norm_gain
):
    vmem = pl.BlockSpec(memory_space=pltpu.VMEM)
    smem = pl.BlockSpec(memory_space=pltpu.SMEM)
    hbm = pl.BlockSpec(memory_space=pl.ANY)
    dma = pltpu.SemaphoreType.DMA
    rows = NX * NZ * SLOTS
    outs = pl.pallas_call(
        decode_kernel,
        out_shape=[jax.ShapeDtypeStruct((SLOTS, WIDTH), BF16)] * 2,
        in_specs=[hbm] * 8 + [smem] * 2,
        out_specs=[vmem, vmem],
        scratch_shapes=[
            pltpu.VMEM((SLOTS, WIDTH), BF16),
            pltpu.VMEM((WIDTH // LANES, LANES), BF16),
            pltpu.VMEM((SLOTS, HEADS, LAT), BF16),
            pltpu.VMEM((SLOTS, ROPE, HEADS), BF16),
            pltpu.VMEM((SLOTS, CTX, LAT), BF16),
            pltpu.VMEM((SLOTS, ROPE, CTX), BF16),
            pltpu.VMEM((LAT // LANES, SLOTS * HEADS, LANES), F32),
            pltpu.VMEM((2, NX - 1, 4, 2, OWN // 2, SLOTS, LAT), BF16),
            pltpu.VMEM((2, 4, NX, 2, OWN // 2, SLOTS, LAT), BF16),
            pltpu.VMEM((NZ, OWN // 2, LAT, 2 * VDIM), BF16),
            pltpu.VMEM((NZ - 1, NX * SLOTS, DEPTH), BF16),
            pltpu.VMEM((NZ, NX * SLOTS, DEPTH), BF16),
            pltpu.VMEM((DEPTH, WIDTH), BF16),
            pltpu.VMEM((4, NZ, NX, SLOTS, XW), BF16),
            pltpu.VMEM((4, NZ, NX, SLOTS, ZW), BF16),
            pltpu.VMEM((4, 3, NZ, SLOTS, XW), BF16),
            pltpu.VMEM((4, 7, SLOTS, XW), BF16),
            pltpu.VMEM((4, 7, NX, SLOTS, ZW), BF16),
            pltpu.VMEM((4, 3, SLOTS, ZW), BF16),
            pltpu.VMEM((SLOTS, 1), F32),
            dma((2,)), dma((4, SLOTS // GROUP)), dma((OWN,)), dma((8,)),
            dma((8,)), dma((8,)), dma((8,)), dma((8,)), dma((16,)), dma((16,)),
            dma((24,)), dma((24,)), dma((7,)), dma((7,)), dma((80,)), dma((80,)),
        ],
        compiler_params=pltpu.CompilerParams(
            collective_id=0, has_side_effects=True, vmem_limit_bytes=56 * 1024 * 1024
        ),
        cost_estimate=pl.CostEstimate(
            flops=2 * rows * DEPTH * WIDTH, bytes_accessed=20 * 1024 * 1024, transcendentals=0
        ),
    )(
        q_latent, q_rope, cache_latent, rope_keys, w_uv, w_o, residual,
        norm_gain.reshape(WIDTH // LANES, LANES), lengths, counts,
    )
    return tuple(outs)


def solution(mesh):
    in_specs = (
        P(("grp", "dp"), None, None),
        P(("grp", "dp"), None, None),
        P(("grp", "dp"), None, None),
        P(("grp", "dp"), None, None),
        P(("grp", "dp")),
        P(("grp", "dp")),
        P("dp", None, None),
        P("dp", None),
        P(("grp", "dp"), None),
        P(),
    )
    out_specs = (P(("grp", "dp"), None), P(("grp", "dp"), None))
    return jax.shard_map(body, mesh=mesh, in_specs=in_specs, out_specs=out_specs, check_vma=False)
```

```python
import jax
import jax.numpy as jnp
from jax import lax
from jax.experimental import pallas as pl
from jax.experimental.pallas import tpu as pltpu
from jax.sharding import PartitionSpec as P

score_scale = 192.0 ** (-0.5)
log2_e = 1.4426950408889634
norm_eps = 1e-06

NX, NY, NZ = 4, 4, 8
SLOTS = 16
HEADS, LAT, VDIM, ROPE, CTX = 128, 512, 128, 64, 512
OWN = 4
WIDTH = 7168
DEPTH = OWN * VDIM
COLS = 256
GROUP = 4
LANES = 128
XW, ZW = 1024, 768
MESH = pl.DeviceIdType.MESH
F32, BF16 = jnp.float32, jnp.bfloat16


def hops(size, kind):
    long, short = size // 2, size // 2 - 1
    return (long, short) if kind == 0 else (short, long)


def decode_kernel(
    q_hbm, qr_hbm, cache_hbm, rope_hbm, wuv_hbm, wo_hbm, res_hbm, gain_hbm, lengths_ref, counts_ref,
    hid_ref, mlp_ref,
    res_ref, gain_ref, q_ref, qr_ref, cache_ref, rope_ref, lat32, lat_out, lat_in, wuv, hv_out, hv,
    wo, px, pz, rx1, rx2, rz1, rz2, acc,
    row_sem, slot_sem, uv_sem, load_sem,
    ring_send, ring_recv, cross_send, cross_recv, pair_send, pair_recv, lat_send, lat_recv, hv_send, hv_recv, send_sem, recv_sem,
):
    dp, grp = lax.axis_index("dp"), lax.axis_index("grp")
    x, z = dp // NZ, dp % NZ
    y, core = grp // 2, grp % 2
    sign = 1 - 2 * core
    sibling = (dp, grp + sign)
    y_pair = y % 2

    def plane(step):
        return (dp, (y + step + NY) % NY * 2 + core)

    def at_x(step):
        return (x + step + NX) % NX

    def at_z(step):
        return (z + step + NZ) % NZ

    def device(dx, dz):
        return (at_x(dx) * NZ + at_z(dz), grp)

    started = []

    def remote(src, dst, sends, recvs, index, target):
        copy = pltpu.make_async_remote_copy(
            src_ref=src, dst_ref=dst, send_sem=sends.at[index], recv_sem=recvs.at[index],
            device_id=target, device_id_type=MESH,
        )
        copy.start()
        started.append(copy)
        return copy

    barrier = pltpu.get_barrier_semaphore()
    peers = [device(d, 0) for d in range(1, NX)] + [device(0, d) for d in range(1, NZ)]
    peers += [sibling, plane(1), plane(-1)]
    for peer in peers:
        pl.semaphore_signal(barrier, inc=1, device_id=peer, device_id_type=MESH)

    def slot_loads(group):
        where = pl.ds(group * GROUP, GROUP)
        return [
            pltpu.make_async_copy(hbm.at[where], vmem.at[where], slot_sem.at[n, group])
            for n, (hbm, vmem) in enumerate(
                ((q_hbm, q_ref), (cache_hbm, cache_ref), (qr_hbm, qr_ref), (rope_hbm, rope_ref))
            )
        ]

    uv_loads = [
        pltpu.make_async_copy(
            wuv_hbm.at[j], wuv.at[z, j // 2, :, pl.ds(j % 2 * VDIM, VDIM)], uv_sem.at[j]
        )
        for j in range(OWN)
    ]
    for load in uv_loads:
        load.start()
    for load in slot_loads(0):
        load.start()
    for group in range(1, SLOTS // GROUP):
        for load in slot_loads(group):
            load.start()
    row_loads = [
        pltpu.make_async_copy(res_hbm, res_ref, row_sem.at[0]),
        pltpu.make_async_copy(gain_hbm, gain_ref, row_sem.at[1]),
    ]
    for load in row_loads:
        load.start()

    streams = []
    for i in range(4):
        streams.append((True, i, i % 2, i * XW, XW))
        streams.append((False, i, i % 2, 4 * XW + i * ZW, ZW))
    loads = []
    for n, (_, _, _, first, width) in enumerate(streams):
        load = pltpu.make_async_copy(
            wo_hbm.at[:, pl.ds(first, width)], wo.at[:, pl.ds(first, width)], load_sem.at[n]
        )
        load.start()
        loads.append(load)

    position = lax.broadcasted_iota(jnp.int32, (1, CTX), 1)

    def score(slot):
        scores = lax.dot_general(
            q_ref[slot], cache_ref[slot], (((1,), (1,)), ((), ())), preferred_element_type=F32
        )
        scores += lax.dot_general(
            qr_ref[slot], rope_ref[slot], (((0,), (0,)), ((), ())), preferred_element_type=F32
        )
        return jnp.where(position < lengths_ref[slot], scores, -1e30)

    def soften(scores):
        top = jnp.max(scores, axis=1, keepdims=True)
        expos = jnp.exp2((scores - top) * (score_scale * log2_e))
        return (expos * (1.0 / jnp.sum(expos, axis=1, keepdims=True))).astype(BF16)

    def gather(slot, probs):
        rows = pl.ds(pl.multiple_of(slot * HEADS, HEADS), HEADS)
        latents = jnp.dot(probs, cache_ref[slot], preferred_element_type=F32)
        for k in range(LAT // LANES):
            lat32[k, rows, :] = latents[:, k * LANES : (k + 1) * LANES]

    def attend_groups(first, last):
        @pl.loop(first, last)
        def _(group):
            for load in slot_loads(group):
                load.wait()
            first = group * GROUP
            scores = [score(first)]
            for j in range(GROUP):
                if j + 1 < GROUP:
                    scores.append(score(first + j + 1))
                gather(first + j, soften(scores[j]))

    ring_hops = (NZ // 2, NZ // 2 - 1)
    ring, pair, cross, cross_pair = {}, {}, {}, {}

    def uv_piece(way, hop, which):
        origin = at_z(hop * (-sign if way == 0 else sign))
        return wuv.at[origin, which, pl.ds(pl.multiple_of(core * (LAT // 2), LAT // 2), LAT // 2)]

    def ring_hop(way, hop):
        to = (x * NZ + at_z(sign if way == 0 else -sign), grp)
        piece = uv_piece(way, hop, y_pair)
        ring[way, hop] = remote(piece, piece, ring_send, ring_recv, way * 4 + hop, to)

    def ring_step(hop):
        for way in (0, 1):
            if hop >= ring_hops[way]:
                continue
            ring[way, hop].wait_recv()
            if hop + 1 < ring_hops[way]:
                ring_hop(way, hop + 1)
            piece = uv_piece(way, hop + 1, y_pair)
            index = way * 4 + hop
            cross[way, hop] = remote(piece, piece, cross_send, cross_recv, index, plane(sign))
            pair[way, hop] = remote(piece, piece, pair_send, pair_recv, index, sibling)

    def cross_step(hop):
        for way in (0, 1):
            if hop >= ring_hops[way]:
                continue
            cross[way, hop].wait_recv()
            piece = uv_piece(way, hop + 1, 1 - y_pair)
            index = 8 + way * 4 + hop
            cross_pair[way, hop] = remote(piece, piece, pair_send, pair_recv, index, sibling)

    order = ((3, -3), (2, -2), (4, 1), (-1, 0))
    moved = {}

    def move_half(half):
        for m, offsets in enumerate(order):
            for step in (1, 3, 2, 0):
                to_x = at_x(step)
                for i, offset in enumerate(offsets):
                    first = (to_x * NZ + at_z(offset * sign)) * OWN
                    for p in range(OWN // 2):
                        for k in range(LAT // LANES):
                            rows = jnp.concatenate(
                                [
                                    lat32[k, pl.ds(half * 8 * HEADS + first + 2 * p + j, 8, stride=HEADS), :]
                                    for j in range(2)
                                ],
                                axis=0,
                            ).astype(BF16)
                            where = pl.ds(k * LANES, LANES)
                            if step == 0:
                                lat_in[half, m, x, i, p, :, where] = rows
                            else:
                                lat_out[half, step - 1, m, i, p, :, where] = rows
                if step > 0:
                    moved[half, m, step] = remote(
                        lat_out.at[half, step - 1, m], lat_in.at[half, m, x], lat_send, lat_recv,
                        (half * 3 + step - 1) * 4 + m, device(step, 0),
                    )

    valued = []

    def head_values(m):
        for half in range(2):
            for step in range(1, NX):
                moved[half, m, step].wait_recv()
        for i, offset in enumerate(order[m]):
            n = 2 * m + i
            to_z = at_z(offset * sign)
            if offset != 0:
                came = (1 if offset < 0 else 0, abs(offset) - 1)
                pair[came].wait_recv()
                cross_pair[came].wait_recv()
            for p in range(OWN // 2):
                rows = lat_in[:, m, :, i, p].reshape(2 * NX * SLOTS, LAT)
                value = jnp.dot(rows, wuv[to_z, p], preferred_element_type=F32)
                value = value.reshape(2, NX, 2, 8, 2 * VDIM)
                for row in range(NX):
                    halves = [
                        jnp.concatenate([value[h, row, 0, :, :VDIM], value[h, row, 1, :, VDIM:]], axis=1)
                        for h in range(2)
                    ]
                    rows = jnp.concatenate(halves, axis=0).astype(BF16)
                    at = (pl.ds(row * SLOTS, SLOTS), pl.ds(p * 2 * VDIM, 2 * VDIM))
                    if offset == 0:
                        hv[z, at[0], at[1]] = rows
                    else:
                        hv_out[n, at[0], at[1]] = rows
            if offset != 0:
                valued.append(
                    remote(hv_out.at[n], hv.at[z], hv_send, hv_recv, n, device(0, offset * sign))
                )

    pl.semaphore_wait(barrier, len(peers))
    for load in uv_loads:
        load.wait()
    ring_hop(0, 0)
    ring_hop(1, 0)
    attend_groups(0, 2)
    ring_step(0)
    move_half(0)
    attend_groups(2, 3)
    ring_step(1)
    cross_step(0)
    attend_groups(3, 4)
    move_half(1)
    cross_step(1)
    ring_step(2)
    cross_step(2)
    ring_step(3)
    cross_step(3)
    for m in range(4):
        head_values(m)
    for copy in valued:
        copy.wait_recv()

    copies = {}

    def send(n, phase, way, hop):
        along_x, i, kind, _, _ = streams[n]
        axis_x = along_x == (phase == 0)
        size = NX if axis_x else NZ
        right, left = hops(size, kind)
        step = right - hop if way == 0 else hop - left
        slot = hop if way == 0 else right + hop
        if along_x:
            part = px.at[i, :, at_x(step)] if phase == 0 else px.at[i, at_z(step), x]
            land = rx1.at[i, slot] if phase == 0 else rx2.at[i, slot]
        else:
            part = pz.at[i, at_z(step)] if phase == 0 else pz.at[i, z, at_x(step)]
            land = rz1.at[i, slot] if phase == 0 else rz2.at[i, slot]
        move = 1 if way == 0 else -1
        if hop > 0:
            copies[n, phase, way, hop - 1][0].wait_recv()
            before = copies[n, phase, way, hop - 1][1]
            part[...] = (before[...].astype(F32) + part[...].astype(F32)).astype(BF16)
        copy = remote(
            part, land, send_sem, recv_sem, len(copies),
            device(move, 0) if axis_x else device(0, move),
        )
        copies[n, phase, way, hop] = (copy, land)

    def first_hops(n, phase):
        for way in (0, 1):
            send(n, phase, way, 0)

    def arrivals(n, phase):
        along_x, _, kind, _, _ = streams[n]
        count = hops(NX if along_x == (phase == 0) else NZ, kind)
        total = None
        for way in (0, 1):
            copy, land = copies[n, phase, way, count[way] - 1]
            copy.wait_recv()
            total = land[...].astype(F32) if total is None else total + land[...].astype(F32)
        return total

    def turn(n):
        along_x, i, _, _, _ = streams[n]
        total = arrivals(n, 0)
        mine = px.at[i, :, x] if along_x else pz.at[i, z]
        mine[...] = (mine[...].astype(F32) + total).astype(BF16)
        first_hops(n, 1)

    live = (
        lax.broadcasted_iota(jnp.int32, (SLOTS, 1), 0) < counts_ref[0]
    ).astype(F32)

    def finish(n):
        along_x, i, _, first, width = streams[n]
        total = arrivals(n, 1)
        mine = px.at[i, z, x] if along_x else pz.at[i, z, x]
        total = total + mine[...].astype(F32)
        where = pl.ds(first, width)
        hidden = (res_ref[:, where].astype(F32) + live * total).astype(BF16)
        hid_ref[:, where] = hidden
        hidden = hidden.astype(F32)
        acc[...] += jnp.sum(hidden * hidden, axis=1, keepdims=True)

    def multiply(n):
        along_x, i, _, first, width = streams[n]
        loads[n].wait()
        part = px if along_x else pz

        @pl.loop(0, width // COLS)
        def _(tile):
            off = pl.multiple_of(tile * COLS, COLS)
            out = jnp.dot(
                hv[...].reshape(NX * NZ * SLOTS, DEPTH), wo[:, pl.ds(first + off, COLS)],
                preferred_element_type=F32,
            )
            part[i, :, :, :, pl.ds(off, COLS)] = out.astype(BF16).reshape(NZ, NX, SLOTS, COLS)

        first_hops(n, 0)

    acc[...] = jnp.zeros_like(acc)
    for load in row_loads:
        load.wait()
    for step in (
        (multiply, 6), (multiply, 7), (multiply, 1), (multiply, 2), (multiply, 5), (multiply, 3),
        (5, 0, 0, 1), (5, 0, 1, 1), (1, 0, 0, 1), (6, 0, 1, 1), (7, 0, 1, 1), (multiply, 0),
        (3, 0, 1, 1), (5, 0, 0, 2), (1, 0, 1, 1), (2, 0, 1, 1), (multiply, 4), (3, 0, 0, 1),
        (3, 0, 1, 2), (5, 0, 0, 3), (7, 0, 0, 1), (7, 0, 1, 2), (1, 0, 1, 2), (1, 0, 0, 2),
        (0, 0, 0, 1), (5, 0, 1, 2), (7, 0, 0, 2), (turn, 6), (7, 0, 1, 3), (4, 0, 0, 1),
        (1, 0, 0, 3), (turn, 5), (turn, 0), (3, 0, 0, 2), (6, 1, 1, 1), (6, 1, 0, 1), (3, 0, 1, 3),
        (turn, 2), (0, 1, 0, 1), (6, 1, 1, 2), (0, 1, 1, 1), (turn, 7), (turn, 4), (turn, 1),
        (2, 1, 1, 1), (2, 1, 0, 1), (turn, 3), (0, 1, 0, 2), (6, 1, 1, 3), (4, 1, 0, 1),
        (1, 1, 0, 1), (2, 1, 0, 2), (2, 1, 1, 2), (4, 1, 1, 1), (5, 1, 0, 1), (0, 1, 0, 3),
        (4, 1, 0, 2), (0, 1, 1, 2), (6, 1, 0, 2), (3, 1, 1, 1), (7, 1, 1, 1), (2, 1, 1, 3),
        (finish, 1), (4, 1, 1, 2), (4, 1, 0, 3), (finish, 0), (finish, 5), (finish, 7), (finish, 2),
        (finish, 6), (finish, 3), (finish, 4),
    ):
        if len(step) == 4:
            send(*step)
        else:
            step[0](step[1])

    inv = lax.rsqrt(acc[...] * (1.0 / WIDTH) + norm_eps)
    gain = gain_ref[...].astype(F32)
    for k in range(WIDTH // LANES):
        where = pl.ds(k * LANES, LANES)
        mlp_ref[:, where] = (hid_ref[:, where].astype(F32) * inv * gain[k : k + 1, :]).astype(BF16)
    for copy in started:
        copy.wait_send()


def body(
    q_latent, q_rope, cache_latent, rope_keys, lengths, counts, w_uv, w_o, residual, norm_gain
):
    vmem = pl.BlockSpec(memory_space=pltpu.VMEM)
    smem = pl.BlockSpec(memory_space=pltpu.SMEM)
    hbm = pl.BlockSpec(memory_space=pl.ANY)
    dma = pltpu.SemaphoreType.DMA
    rows = NX * NZ * SLOTS
    outs = pl.pallas_call(
        decode_kernel,
        out_shape=[jax.ShapeDtypeStruct((SLOTS, WIDTH), BF16)] * 2,
        in_specs=[hbm] * 8 + [smem] * 2,
        out_specs=[vmem, vmem],
        scratch_shapes=[
            pltpu.VMEM((SLOTS, WIDTH), BF16),
            pltpu.VMEM((WIDTH // LANES, LANES), BF16),
            pltpu.VMEM((SLOTS, HEADS, LAT), BF16),
            pltpu.VMEM((SLOTS, ROPE, HEADS), BF16),
            pltpu.VMEM((SLOTS, CTX, LAT), BF16),
            pltpu.VMEM((SLOTS, ROPE, CTX), BF16),
            pltpu.VMEM((LAT // LANES, SLOTS * HEADS, LANES), F32),
            pltpu.VMEM((2, NX - 1, 4, 2, OWN // 2, SLOTS, LAT), BF16),
            pltpu.VMEM((2, 4, NX, 2, OWN // 2, SLOTS, LAT), BF16),
            pltpu.VMEM((NZ, OWN // 2, LAT, 2 * VDIM), BF16),
            pltpu.VMEM((NZ - 1, NX * SLOTS, DEPTH), BF16),
            pltpu.VMEM((NZ, NX * SLOTS, DEPTH), BF16),
            pltpu.VMEM((DEPTH, WIDTH), BF16),
            pltpu.VMEM((4, NZ, NX, SLOTS, XW), BF16),
            pltpu.VMEM((4, NZ, NX, SLOTS, ZW), BF16),
            pltpu.VMEM((4, 3, NZ, SLOTS, XW), BF16),
            pltpu.VMEM((4, 7, SLOTS, XW), BF16),
            pltpu.VMEM((4, 7, NX, SLOTS, ZW), BF16),
            pltpu.VMEM((4, 3, SLOTS, ZW), BF16),
            pltpu.VMEM((SLOTS, 1), F32),
            dma((2,)), dma((4, SLOTS // GROUP)), dma((OWN,)), dma((8,)),
            dma((8,)), dma((8,)), dma((8,)), dma((8,)), dma((16,)), dma((16,)),
            dma((24,)), dma((24,)), dma((7,)), dma((7,)), dma((80,)), dma((80,)),
        ],
        compiler_params=pltpu.CompilerParams(
            collective_id=0, has_side_effects=True, vmem_limit_bytes=52 * 1024 * 1024
        ),
        cost_estimate=pl.CostEstimate(
            flops=2 * rows * DEPTH * WIDTH, bytes_accessed=20 * 1024 * 1024, transcendentals=0
        ),
    )(
        q_latent, q_rope, cache_latent, rope_keys, w_uv, w_o, residual,
        norm_gain.reshape(WIDTH // LANES, LANES), lengths, counts,
    )
    return tuple(outs)


def solution(mesh):
    in_specs = (
        P(("grp", "dp"), None, None),
        P(("grp", "dp"), None, None),
        P(("grp", "dp"), None, None),
        P(("grp", "dp"), None, None),
        P(("grp", "dp")),
        P(("grp", "dp")),
        P("dp", None, None),
        P("dp", None),
        P(("grp", "dp"), None),
        P(),
    )
    out_specs = (P(("grp", "dp"), None), P(("grp", "dp"), None))
    return jax.shard_map(body, mesh=mesh, in_specs=in_specs, out_specs=out_specs, check_vma=False)
```

```python
import jax
import jax.numpy as jnp
from jax import lax
from jax.experimental import pallas as pl
from jax.experimental.pallas import tpu as pltpu
from jax.sharding import PartitionSpec as P

score_scale = 192.0 ** (-0.5)
log2_e = 1.4426950408889634
norm_eps = 1e-06

NX, NY, NZ = 4, 4, 8
SLOTS = 16
HEADS, LAT, VDIM, ROPE, CTX = 128, 512, 128, 64, 512
OWN = 4
WIDTH = 7168
DEPTH = OWN * VDIM
COLS = 256
GROUP = 4
LANES = 128
XW, ZW = 1024, 768
MESH = pl.DeviceIdType.MESH
F32, BF16 = jnp.float32, jnp.bfloat16


def hops(size, kind):
    long, short = size // 2, size // 2 - 1
    return (long, short) if kind == 0 else (short, long)


def decode_kernel(
    q_hbm, qr_hbm, cache_hbm, rope_hbm, wuv_hbm, wo_hbm, res_hbm, gain_hbm, lengths_ref, counts_ref,
    hid_ref, mlp_ref,
    res_ref, gain_ref, q_ref, qr_ref, cache_ref, rope_ref, lat32, lat_out, lat_in, wuv, hv_out, hv,
    wo, px, pz, rx1, rx2, rz1, rz2, acc,
    row_sem, slot_sem, uv_sem, load_sem,
    ring_send, ring_recv, cross_send, cross_recv, pair_send, pair_recv, lat_send, lat_recv, hv_send, hv_recv, send_sem, recv_sem,
):
    dp, grp = lax.axis_index("dp"), lax.axis_index("grp")
    x, z = dp // NZ, dp % NZ
    y, core = grp // 2, grp % 2
    sign = 1 - 2 * core
    sibling = (dp, grp + sign)
    y_pair = y % 2

    def plane(step):
        return (dp, (y + step + NY) % NY * 2 + core)

    def at_x(step):
        return (x + step + NX) % NX

    def at_z(step):
        return (z + step + NZ) % NZ

    def device(dx, dz):
        return (at_x(dx) * NZ + at_z(dz), grp)

    started = []

    def remote(src, dst, sends, recvs, index, target):
        copy = pltpu.make_async_remote_copy(
            src_ref=src, dst_ref=dst, send_sem=sends.at[index], recv_sem=recvs.at[index],
            device_id=target, device_id_type=MESH,
        )
        copy.start()
        started.append(copy)
        return copy

    barrier = pltpu.get_barrier_semaphore()
    peers = [device(d, 0) for d in range(1, NX)] + [device(0, d) for d in range(1, NZ)]
    peers += [sibling, plane(1), plane(-1)]
    for peer in peers:
        pl.semaphore_signal(barrier, inc=1, device_id=peer, device_id_type=MESH)

    def slot_loads(group):
        where = pl.ds(group * GROUP, GROUP)
        return [
            pltpu.make_async_copy(hbm.at[where], vmem.at[where], slot_sem.at[n, group])
            for n, (hbm, vmem) in enumerate(
                ((q_hbm, q_ref), (cache_hbm, cache_ref), (qr_hbm, qr_ref), (rope_hbm, rope_ref))
            )
        ]

    for load in slot_loads(0):
        load.start()
    uv_loads = [
        pltpu.make_async_copy(
            wuv_hbm.at[j], wuv.at[z, j // 2, :, pl.ds(j % 2 * VDIM, VDIM)], uv_sem.at[j]
        )
        for j in range(OWN)
    ]
    for load in uv_loads:
        load.start()
    for group in range(1, SLOTS // GROUP):
        for load in slot_loads(group):
            load.start()
    row_loads = [
        pltpu.make_async_copy(res_hbm, res_ref, row_sem.at[0]),
        pltpu.make_async_copy(gain_hbm, gain_ref, row_sem.at[1]),
    ]
    for load in row_loads:
        load.start()

    streams = []
    for i in range(4):
        streams.append((True, i, i % 2, i * XW, XW))
        streams.append((False, i, i % 2, 4 * XW + i * ZW, ZW))
    loads = []
    for n, (_, _, _, first, width) in enumerate(streams):
        load = pltpu.make_async_copy(
            wo_hbm.at[:, pl.ds(first, width)], wo.at[:, pl.ds(first, width)], load_sem.at[n]
        )
        load.start()
        loads.append(load)

    position = lax.broadcasted_iota(jnp.int32, (1, CTX), 1)

    def score(slot):
        scores = lax.dot_general(
            q_ref[slot], cache_ref[slot], (((1,), (1,)), ((), ())), preferred_element_type=F32
        )
        scores += lax.dot_general(
            qr_ref[slot], rope_ref[slot], (((0,), (0,)), ((), ())), preferred_element_type=F32
        )
        return jnp.where(position < lengths_ref[slot], scores, -1e30)

    def soften(scores):
        top = jnp.max(scores, axis=1, keepdims=True)
        expos = jnp.exp2((scores - top) * (score_scale * log2_e))
        return (expos * (1.0 / jnp.sum(expos, axis=1, keepdims=True))).astype(BF16)

    def gather(slot, probs):
        rows = pl.ds(pl.multiple_of(slot * HEADS, HEADS), HEADS)
        latents = jnp.dot(probs, cache_ref[slot], preferred_element_type=F32)
        for k in range(LAT // LANES):
            lat32[k, rows, :] = latents[:, k * LANES : (k + 1) * LANES]

    def attend_groups(first, last):
        @pl.loop(first, last)
        def _(group):
            for load in slot_loads(group):
                load.wait()
            first = group * GROUP
            scores = [score(first)]
            for j in range(GROUP):
                if j + 1 < GROUP:
                    scores.append(score(first + j + 1))
                gather(first + j, soften(scores[j]))

    ring_hops = (NZ // 2, NZ // 2 - 1)
    ring, pair, cross, cross_pair = {}, {}, {}, {}

    def uv_piece(way, hop, which):
        origin = at_z(hop * (-sign if way == 0 else sign))
        return wuv.at[origin, which, pl.ds(pl.multiple_of(core * (LAT // 2), LAT // 2), LAT // 2)]

    def ring_hop(way, hop):
        to = (x * NZ + at_z(sign if way == 0 else -sign), grp)
        piece = uv_piece(way, hop, y_pair)
        ring[way, hop] = remote(piece, piece, ring_send, ring_recv, way * 4 + hop, to)

    def ring_step(hop):
        for way in (0, 1):
            if hop >= ring_hops[way]:
                continue
            ring[way, hop].wait_recv()
            if hop + 1 < ring_hops[way]:
                ring_hop(way, hop + 1)
            piece = uv_piece(way, hop + 1, y_pair)
            index = way * 4 + hop
            cross[way, hop] = remote(piece, piece, cross_send, cross_recv, index, plane(sign))
            pair[way, hop] = remote(piece, piece, pair_send, pair_recv, index, sibling)

    def cross_step(hop):
        for way in (0, 1):
            if hop >= ring_hops[way]:
                continue
            cross[way, hop].wait_recv()
            piece = uv_piece(way, hop + 1, 1 - y_pair)
            index = 8 + way * 4 + hop
            cross_pair[way, hop] = remote(piece, piece, pair_send, pair_recv, index, sibling)

    order = ((3, -3), (2, -2), (4, 1), (-1, 0))
    moved = {}

    def move_half(half):
        for m, offsets in enumerate(order):
            for step in (1, 3, 2, 0):
                to_x = at_x(step)
                for i, offset in enumerate(offsets):
                    first = (to_x * NZ + at_z(offset * sign)) * OWN
                    for p in range(OWN // 2):
                        for k in range(LAT // LANES):
                            rows = jnp.concatenate(
                                [
                                    lat32[k, pl.ds(half * 8 * HEADS + first + 2 * p + j, 8, stride=HEADS), :]
                                    for j in range(2)
                                ],
                                axis=0,
                            ).astype(BF16)
                            where = pl.ds(k * LANES, LANES)
                            if step == 0:
                                lat_in[half, m, x, i, p, :, where] = rows
                            else:
                                lat_out[half, step - 1, m, i, p, :, where] = rows
                if step > 0:
                    moved[half, m, step] = remote(
                        lat_out.at[half, step - 1, m], lat_in.at[half, m, x], lat_send, lat_recv,
                        (half * 3 + step - 1) * 4 + m, device(step, 0),
                    )

    valued = []

    def head_values(m):
        for half in range(2):
            for step in range(1, NX):
                moved[half, m, step].wait_recv()
        for i, offset in enumerate(order[m]):
            n = 2 * m + i
            to_z = at_z(offset * sign)
            if offset != 0:
                came = (1 if offset < 0 else 0, abs(offset) - 1)
                pair[came].wait_recv()
                cross_pair[came].wait_recv()
            for p in range(OWN // 2):
                rows = lat_in[:, m, :, i, p].reshape(2 * NX * SLOTS, LAT)
                value = jnp.dot(rows, wuv[to_z, p], preferred_element_type=F32)
                value = value.reshape(2, NX, 2, 8, 2 * VDIM)
                for row in range(NX):
                    halves = [
                        jnp.concatenate([value[h, row, 0, :, :VDIM], value[h, row, 1, :, VDIM:]], axis=1)
                        for h in range(2)
                    ]
                    rows = jnp.concatenate(halves, axis=0).astype(BF16)
                    at = (pl.ds(row * SLOTS, SLOTS), pl.ds(p * 2 * VDIM, 2 * VDIM))
                    if offset == 0:
                        hv[z, at[0], at[1]] = rows
                    else:
                        hv_out[n, at[0], at[1]] = rows
            if offset != 0:
                valued.append(
                    remote(hv_out.at[n], hv.at[z], hv_send, hv_recv, n, device(0, offset * sign))
                )

    attend_groups(0, 1)
    pl.semaphore_wait(barrier, len(peers))
    for load in uv_loads:
        load.wait()
    ring_hop(0, 0)
    ring_hop(1, 0)
    attend_groups(1, 2)
    move_half(0)
    attend_groups(2, 3)
    ring_step(0)
    attend_groups(3, 4)
    move_half(1)
    ring_step(1)
    cross_step(0)
    ring_step(2)
    cross_step(1)
    cross_step(2)
    ring_step(3)
    head_values(0)
    cross_step(3)
    for m in range(1, 4):
        head_values(m)
    for copy in valued:
        copy.wait_recv()

    copies = {}

    def send(n, phase, way, hop):
        along_x, i, kind, _, _ = streams[n]
        axis_x = along_x == (phase == 0)
        size = NX if axis_x else NZ
        right, left = hops(size, kind)
        step = right - hop if way == 0 else hop - left
        slot = hop if way == 0 else right + hop
        if along_x:
            part = px.at[i, :, at_x(step)] if phase == 0 else px.at[i, at_z(step), x]
            land = rx1.at[i, slot] if phase == 0 else rx2.at[i, slot]
        else:
            part = pz.at[i, at_z(step)] if phase == 0 else pz.at[i, z, at_x(step)]
            land = rz1.at[i, slot] if phase == 0 else rz2.at[i, slot]
        move = 1 if way == 0 else -1
        if hop > 0:
            copies[n, phase, way, hop - 1][0].wait_recv()
            before = copies[n, phase, way, hop - 1][1]
            part[...] = (before[...].astype(F32) + part[...].astype(F32)).astype(BF16)
        copy = remote(
            part, land, send_sem, recv_sem, len(copies),
            device(move, 0) if axis_x else device(0, move),
        )
        copies[n, phase, way, hop] = (copy, land)

    def first_hops(n, phase):
        for way in (0, 1):
            send(n, phase, way, 0)

    def arrivals(n, phase):
        along_x, _, kind, _, _ = streams[n]
        count = hops(NX if along_x == (phase == 0) else NZ, kind)
        total = None
        for way in (0, 1):
            copy, land = copies[n, phase, way, count[way] - 1]
            copy.wait_recv()
            total = land[...].astype(F32) if total is None else total + land[...].astype(F32)
        return total

    def turn(n):
        along_x, i, _, _, _ = streams[n]
        total = arrivals(n, 0)
        mine = px.at[i, :, x] if along_x else pz.at[i, z]
        mine[...] = (mine[...].astype(F32) + total).astype(BF16)
        first_hops(n, 1)

    live = (
        lax.broadcasted_iota(jnp.int32, (SLOTS, 1), 0) < counts_ref[0]
    ).astype(F32)

    def finish(n):
        along_x, i, _, first, width = streams[n]
        total = arrivals(n, 1)
        mine = px.at[i, z, x] if along_x else pz.at[i, z, x]
        total = total + mine[...].astype(F32)
        where = pl.ds(first, width)
        hidden = (res_ref[:, where].astype(F32) + live * total).astype(BF16)
        hid_ref[:, where] = hidden
        hidden = hidden.astype(F32)
        acc[...] += jnp.sum(hidden * hidden, axis=1, keepdims=True)

    def multiply(n):
        along_x, i, _, first, width = streams[n]
        loads[n].wait()
        part = px if along_x else pz

        @pl.loop(0, width // COLS)
        def _(tile):
            off = pl.multiple_of(tile * COLS, COLS)
            out = jnp.dot(
                hv[...].reshape(NX * NZ * SLOTS, DEPTH), wo[:, pl.ds(first + off, COLS)],
                preferred_element_type=F32,
            )
            part[i, :, :, :, pl.ds(off, COLS)] = out.astype(BF16).reshape(NZ, NX, SLOTS, COLS)

        first_hops(n, 0)

    acc[...] = jnp.zeros_like(acc)
    for load in row_loads:
        load.wait()
    for step in (
        (multiply, 6), (multiply, 7), (multiply, 1), (multiply, 2), (multiply, 5), (multiply, 3),
        (5, 0, 0, 1), (5, 0, 1, 1), (1, 0, 0, 1), (6, 0, 1, 1), (7, 0, 1, 1), (multiply, 0),
        (3, 0, 1, 1), (5, 0, 0, 2), (1, 0, 1, 1), (2, 0, 1, 1), (multiply, 4), (3, 0, 0, 1),
        (3, 0, 1, 2), (5, 0, 0, 3), (7, 0, 0, 1), (7, 0, 1, 2), (1, 0, 1, 2), (1, 0, 0, 2),
        (0, 0, 0, 1), (5, 0, 1, 2), (7, 0, 0, 2), (turn, 6), (7, 0, 1, 3), (4, 0, 0, 1),
        (1, 0, 0, 3), (turn, 5), (turn, 0), (3, 0, 0, 2), (6, 1, 1, 1), (6, 1, 0, 1), (3, 0, 1, 3),
        (turn, 2), (0, 1, 0, 1), (6, 1, 1, 2), (0, 1, 1, 1), (turn, 7), (turn, 4), (turn, 1),
        (2, 1, 1, 1), (2, 1, 0, 1), (turn, 3), (0, 1, 0, 2), (6, 1, 1, 3), (4, 1, 0, 1),
        (1, 1, 0, 1), (2, 1, 0, 2), (2, 1, 1, 2), (4, 1, 1, 1), (5, 1, 0, 1), (0, 1, 0, 3),
        (4, 1, 0, 2), (0, 1, 1, 2), (6, 1, 0, 2), (3, 1, 1, 1), (7, 1, 1, 1), (2, 1, 1, 3),
        (finish, 1), (4, 1, 1, 2), (4, 1, 0, 3), (finish, 0), (finish, 5), (finish, 7), (finish, 2),
        (finish, 6), (finish, 3), (finish, 4),
    ):
        if len(step) == 4:
            send(*step)
        else:
            step[0](step[1])

    inv = lax.rsqrt(acc[...] * (1.0 / WIDTH) + norm_eps)
    gain = gain_ref[...].astype(F32)
    for k in range(WIDTH // LANES):
        where = pl.ds(k * LANES, LANES)
        mlp_ref[:, where] = (hid_ref[:, where].astype(F32) * inv * gain[k : k + 1, :]).astype(BF16)
    for copy in started:
        copy.wait_send()


def body(
    q_latent, q_rope, cache_latent, rope_keys, lengths, counts, w_uv, w_o, residual, norm_gain
):
    vmem = pl.BlockSpec(memory_space=pltpu.VMEM)
    smem = pl.BlockSpec(memory_space=pltpu.SMEM)
    hbm = pl.BlockSpec(memory_space=pl.ANY)
    dma = pltpu.SemaphoreType.DMA
    rows = NX * NZ * SLOTS
    outs = pl.pallas_call(
        decode_kernel,
        out_shape=[jax.ShapeDtypeStruct((SLOTS, WIDTH), BF16)] * 2,
        in_specs=[hbm] * 8 + [smem] * 2,
        out_specs=[vmem, vmem],
        scratch_shapes=[
            pltpu.VMEM((SLOTS, WIDTH), BF16),
            pltpu.VMEM((WIDTH // LANES, LANES), BF16),
            pltpu.VMEM((SLOTS, HEADS, LAT), BF16),
            pltpu.VMEM((SLOTS, ROPE, HEADS), BF16),
            pltpu.VMEM((SLOTS, CTX, LAT), BF16),
            pltpu.VMEM((SLOTS, ROPE, CTX), BF16),
            pltpu.VMEM((LAT // LANES, SLOTS * HEADS, LANES), F32),
            pltpu.VMEM((2, NX - 1, 4, 2, OWN // 2, SLOTS, LAT), BF16),
            pltpu.VMEM((2, 4, NX, 2, OWN // 2, SLOTS, LAT), BF16),
            pltpu.VMEM((NZ, OWN // 2, LAT, 2 * VDIM), BF16),
            pltpu.VMEM((NZ - 1, NX * SLOTS, DEPTH), BF16),
            pltpu.VMEM((NZ, NX * SLOTS, DEPTH), BF16),
            pltpu.VMEM((DEPTH, WIDTH), BF16),
            pltpu.VMEM((4, NZ, NX, SLOTS, XW), BF16),
            pltpu.VMEM((4, NZ, NX, SLOTS, ZW), BF16),
            pltpu.VMEM((4, 3, NZ, SLOTS, XW), BF16),
            pltpu.VMEM((4, 7, SLOTS, XW), BF16),
            pltpu.VMEM((4, 7, NX, SLOTS, ZW), BF16),
            pltpu.VMEM((4, 3, SLOTS, ZW), BF16),
            pltpu.VMEM((SLOTS, 1), F32),
            dma((2,)), dma((4, SLOTS // GROUP)), dma((OWN,)), dma((8,)),
            dma((8,)), dma((8,)), dma((8,)), dma((8,)), dma((16,)), dma((16,)),
            dma((24,)), dma((24,)), dma((7,)), dma((7,)), dma((80,)), dma((80,)),
        ],
        compiler_params=pltpu.CompilerParams(
            collective_id=0, has_side_effects=True, vmem_limit_bytes=52 * 1024 * 1024
        ),
        cost_estimate=pl.CostEstimate(
            flops=2 * rows * DEPTH * WIDTH, bytes_accessed=20 * 1024 * 1024, transcendentals=0
        ),
    )(
        q_latent, q_rope, cache_latent, rope_keys, w_uv, w_o, residual,
        norm_gain.reshape(WIDTH // LANES, LANES), lengths, counts,
    )
    return tuple(outs)


def solution(mesh):
    in_specs = (
        P(("grp", "dp"), None, None),
        P(("grp", "dp"), None, None),
        P(("grp", "dp"), None, None),
        P(("grp", "dp"), None, None),
        P(("grp", "dp")),
        P(("grp", "dp")),
        P("dp", None, None),
        P("dp", None),
        P(("grp", "dp"), None),
        P(),
    )
    out_specs = (P(("grp", "dp"), None), P(("grp", "dp"), None))
    return jax.shard_map(body, mesh=mesh, in_specs=in_specs, out_specs=out_specs, check_vma=False)
```
